256 devices in a mesh: dp: 16 (over z_lo, y, core), seq: 16 (over z_hi, x).
Axes of the slice: x: 4, y: 4, z: 8 (z_hi: 4, z_lo: 2; z = z_hi * 2 + z_lo), core: 2. Of those that a mesh axis runs over, the one named last changes fastest.
Arguments:
- inputs: bfloat16 [16, 2048, 6144], P('dp', 'seq'), may hold values from -6 to 6
- queries: bfloat16 [16, 2048, 3072], P('dp', 'seq'), may hold values from -12 to 12
- values: bfloat16 [16, 2048, 512], P('dp', 'seq'), may hold values from -6 to 6
- key_weight: bfloat16 [6144, 512], P('seq'), may hold values from -0.078125 to 0.078125
- doc_ids: int32 [16, 2048], P('dp'), may hold values from 0 to 7, never falling along the last dimension, each value on 1 to 1024 neighbouring positions
- grad_out: bfloat16 [16, 2048, 3072], P('dp', 'seq'), may hold values from -24 to 24
Outputs:
- attn_out: bfloat16 [16, 2048, 3072], P('dp', 'seq')
- grad_queries: bfloat16 [16, 2048, 3072], P('dp', 'seq')
- grad_values: bfloat16 [16, 2048, 512], P('dp', 'seq')
- grad_key_weight: float32 [6144, 512], P('seq')
The draws below stay inside these ranges and needn't reach their ends.
Inputs may be any that keep to these rules, and one draw needn't show every extreme that they name: `doc_ids`: along each window the document number never falls; each document holds 1 to 1024 tokens and one holds exactly 1024.
All inputs are finite; a program needn't handle non-finite values.
Results may differ from the reference program's by a relative error of at most 0.02.
Values may be sent and summed in bfloat16 or wider, within the bound.
A program may use at most 128 MiB of HBM per device.

```python
import math
import jax
import jax.numpy as jnp
import numpy as np
from jax import lax

D = 6144
QH = 24
KVH = 4
HD = 128
DOCS = 8
QW = 3072
KVW = 512
TOKENS = 2048
WINDOWS = 16
DOC_MOST = 1024


def level_of(key, extent, split, least, largest):
    gain = 1.0
    for axis_at, parts in split:
        steps = jax.random.uniform(jax.random.fold_in(jax.random.fold_in(key, 6), axis_at), (parts,), jnp.float32, least / len(split), largest / len(split))
        gain = gain * jnp.repeat(jnp.exp(steps), extent[axis_at] // parts).reshape((-1,) + (1,) * (len(extent) - 1 - axis_at))
    return gain


def length_profile(count, total, reach, skew):
    loads = [(1 << 20) // math.isqrt(grade ** skew) + 1 for grade in range(2, count + 1)]
    rest, given = total - reach - (count - 1), [1] * (count - 1)
    while rest > 0:
        free = [i for i in range(count - 1) if given[i] < reach]
        pool, remaining = sum([loads[i] for i in free]), rest
        for i in free:
            extra = min(reach - given[i], max(1, remaining * loads[i] // pool), rest)
            given[i] = given[i] + extra
            rest = rest - extra
    return np.array([reach] + given)


def uneven(stream_key, number_of, total, limit, skew):
    if number_of == 2:
        one = jax.random.randint(stream_key, (), max(1, total - limit), min(limit, total - 1) + 1)
        return jnp.stack([one, total - one])
    sizes = jnp.asarray(length_profile(number_of, total, limit, skew), jnp.int32)
    pairs = (number_of - 1) // 2
    source_of, sink = sizes[1:1 + 2 * pairs:2], sizes[2:2 + 2 * pairs:2]
    slack = jnp.minimum(source_of - 1, limit - sink)
    shifted = jax.random.randint(jax.random.fold_in(stream_key, 1), (pairs,), 0, 1 << 20) % (slack + 1)
    sizes = sizes.at[1:1 + 2 * pairs:2].set(source_of - shifted).at[2:2 + 2 * pairs:2].set(sink + shifted)
    return sizes[jax.random.permutation(jax.random.fold_in(stream_key, 2), number_of)]


def bell_draw(rng, shape, scale, most, pieces=(), dtype=jnp.bfloat16):
    loudness = level_of(rng, shape, pieces, -0.22, 0.18) if pieces else 1.0
    drawn = jax.random.normal(rng, shape, jnp.float32) * scale * loudness
    return jnp.minimum(jnp.maximum(drawn, -most), most).astype(dtype)


def setup_inputs(seed: int = 0) -> dict:
    arg_keys = jax.random.split(jax.random.key(seed), 7)
    return {
        "inputs": bell_draw(arg_keys[0], (WINDOWS, TOKENS, D), 1.0, 6.0, ((0, 16), (1, 16))),
        "queries": bell_draw(arg_keys[1], (WINDOWS, TOKENS, QW), 2.0, 12.0, ((0, 16), (1, 16))),
        "values": bell_draw(arg_keys[2], (WINDOWS, TOKENS, KVW), 1.0, 6.0, ((0, 16), (1, 16))),
        "key_weight": bell_draw(arg_keys[3], (D, KVW), D ** -0.5, 0.078125, ((0, 16),)),
        "doc_ids": jax.vmap(lambda own: jnp.searchsorted(jnp.cumsum(uneven(own, DOCS, TOKENS, DOC_MOST, 2)), jnp.arange(TOKENS), side="right"))(jax.random.split(arg_keys[4], WINDOWS)).reshape((WINDOWS, TOKENS)).astype(jnp.int32),
        "grad_out": bell_draw(arg_keys[5], (WINDOWS, TOKENS, QW), 4.0, 24.0, ((0, 16), (1, 16))),
    }


ROPE_BASE = 1000000.0

def rotate(field, position, heads, sign):
    count = field.shape[0]
    width = field.shape[1] // heads
    half = width // 2
    shaped = field.reshape(count, heads, width)
    freqs = ROPE_BASE ** (-(jnp.arange(half).astype(jnp.float32) * 2.0 / width))
    angles = position.astype(jnp.float32)[:, None] * freqs[None, :]
    cosine = jnp.cos(angles)[:, None, :]
    sine = jnp.sin(angles)[:, None, :]
    first = shaped[..., :half]
    second = shaped[..., half:]
    out_first = first * cosine - sign * second * sine
    out_second = sign * first * sine + second * cosine
    return jnp.concatenate([out_first, out_second], axis=-1).reshape(count, heads * width)

def rounded(array):
    return lax.optimization_barrier(array.astype(jnp.bfloat16)).astype(jnp.float32)

def window(inputs, queries, values, key_weight, docs, grad_out):
    group = QH // KVH
    scale = 1.0 / math.sqrt(HD)
    positions = jnp.arange(TOKENS).astype(jnp.int32)
    key_raw = jnp.dot(inputs, key_weight, preferred_element_type=jnp.float32)
    keys = rotate(key_raw, positions, KVH, 1.0).astype(jnp.bfloat16)
    key_heads = keys.reshape(TOKENS, KVH, HD).astype(jnp.float32)
    value_heads = values.reshape(TOKENS, KVH, HD).astype(jnp.float32)
    tile = math.gcd(TOKENS, 512)
    count = TOKENS // tile
    query_tiles = queries.reshape(count, tile, KVH, group, HD)
    cot_tiles = grad_out.reshape(count, tile, KVH, group, HD)
    doc_tiles = docs.reshape(count, tile)
    pos_tiles = positions.reshape(count, tile)

    def step(carry, item):
        query_tile, cot_tile, doc_tile, pos_tile = item
        query_float = query_tile.astype(jnp.float32)
        scores = jnp.einsum('tkgd,ckd->kgtc', query_float, key_heads) * scale
        visible = (doc_tile[:, None] == docs[None, :]) & (pos_tile[:, None] >= positions[None, :])
        weights = jnp.where(visible[None, None], jnp.exp(scores), 0.0)
        sums = lax.optimization_barrier(jnp.sum(weights, axis=-1))
        mixed = jnp.einsum('kgtc,ckd->tkgd', rounded(weights), value_heads)
        attended = (mixed / jnp.transpose(sums, (2, 0, 1))[..., None]).astype(jnp.bfloat16)
        cot_float = cot_tile.astype(jnp.float32)
        delta = jnp.transpose(lax.optimization_barrier(jnp.sum(cot_float * attended.astype(jnp.float32), axis=-1)), (1, 2, 0))
        probs = weights / sums[..., None]
        dvalue = jnp.einsum('kgtc,tkgd->ckd', rounded(probs), cot_float)
        dprobs = jnp.einsum('tkgd,ckd->kgtc', cot_float, value_heads)
        dscores = rounded(probs * (dprobs - delta[..., None]))
        dquery = jnp.einsum('kgtc,ckd->tkgd', dscores, key_heads) * scale
        dkey = jnp.einsum('kgtc,tkgd->ckd', dscores, query_float) * scale
        return ((carry[0] + dkey, carry[1] + dvalue), (attended, dquery.astype(jnp.bfloat16)))
    zeros = jnp.zeros((TOKENS, KVH, HD), jnp.float32)
    (dkey_all, dvalue_all), (attended_tiles, dquery_tiles) = lax.scan(step, (zeros, zeros), (query_tiles, cot_tiles, doc_tiles, pos_tiles))
    key_grad_raw = rotate(dkey_all.reshape(TOKENS, KVH * HD), positions, KVH, -1.0).astype(jnp.bfloat16)
    partial_grad = jnp.dot(inputs.T, key_grad_raw, preferred_element_type=jnp.float32)
    return (attended_tiles.reshape(TOKENS, QH * HD), dquery_tiles.reshape(TOKENS, QH * HD), dvalue_all.reshape(TOKENS, KVH * HD).astype(jnp.bfloat16), partial_grad)

def reference(inputs, queries, values, key_weight, doc_ids, grad_out):

    def single(bundle):
        return window(bundle[0], bundle[1], bundle[2], key_weight, bundle[3], bundle[4])
    attn_out, grad_queries, grad_values, partial_grads = lax.map(single, (inputs, queries, values, doc_ids, grad_out))
    grad_key_weight = lax.optimization_barrier(jnp.sum(partial_grads, axis=0)) / WINDOWS
    return (attn_out, grad_queries, grad_values, grad_key_weight)
```

```python
import math

import jax
import jax.numpy as jnp
from jax import lax
from jax.experimental import pallas as pl
from jax.experimental.pallas import tpu as pltpu
from jax.sharding import PartitionSpec as P

QH = 24
KVH = 4
HD = 128
GROUP = QH // KVH
ROPE_BASE = 1000000.0
MESH = pl.DeviceIdType.MESH
BF = jnp.bfloat16
F32 = jnp.float32
NQ = 4
VMEM_LIMIT = 56 * 1024 * 1024


class Place:
    def __init__(self):
        dp = lax.axis_index("dp")
        sq = lax.axis_index("seq")
        self.lo = dp // 8
        self.y = (dp // 2) % 4
        self.c = dp % 2
        self.zh = sq // 4
        self.x = sq % 4
        self.j = dp % 8

    def at(self, lo=None, y=None, c=None, zh=None, x=None):
        lo = self.lo if lo is None else lo
        y = self.y if y is None else y
        c = self.c if c is None else c
        zh = self.zh if zh is None else zh
        x = self.x if x is None else x
        return (lo * 8 + y * 2 + c, zh * 4 + x)

    def z_next(self):
        return self.at(lo=1 - self.lo, zh=(self.zh + self.lo) % 4)

    def z_prev(self):
        return self.at(lo=1 - self.lo, zh=(self.zh + 3 + self.lo) % 4)


class Copies:
    def __init__(self, send, recv):
        self.send, self.recv, self.count = send, recv, 0

    def new(self, number=1):
        first = self.count
        self.count += number
        return first

    def make(self, src, dst, index, device):
        return pltpu.make_async_remote_copy(
            src_ref=src,
            dst_ref=dst,
            send_sem=self.send.at[index],
            recv_sem=self.recv.at[index],
            device_id=device,
            device_id_type=MESH,
        )


def greet(devices):
    barrier = pltpu.get_barrier_semaphore()
    for device in devices:
        pl.semaphore_signal(barrier, inc=1, device_id=device, device_id_type=MESH)
    pl.semaphore_wait(barrier, len(devices))


def kind(source, reader):
    return jnp.where(reader > source, 0, 2)


class Gather:
    def __init__(self, place, copies, buf):
        self.p, self.copies, self.buf = place, copies, buf
        p = place
        x = p.x
        self.xl, self.xr = (x + 3) % 4, (x + 1) % 4
        self.left, self.right = p.at(x=self.xl), p.at(x=self.xr)
        self.up = p.at(zh=(p.zh + 1) % 4)
        self.kr, self.kl = kind(x, self.xr), kind(x, self.xl)
        self.fr = jnp.where(self.xl < 2, kind(self.xl, self.xr), 1)
        self.fl = jnp.where(self.xr < 2, 1, kind(self.xr, self.xl))
        self.base = copies.new(16)
        self.sent = []

    def cp(self, what, h, xs, k, device):
        at = pl.ds(256 * h, 256)
        to = k + 1 if what < 2 else k
        return self.copies.make(
            self.buf.at[xs, k, :, at], self.buf.at[xs, to, :, at], self.base + 2 * what + h, device
        )

    def z1(self, h):
        x = self.p.x
        c = self.cp(0, h, x, 0, self.up)
        c.start()
        for what, k, dev in ((4, self.kr, self.right), (5, self.kl, self.left)):
            @pl.when(k == 0)
            def _():
                self.cp(what, h, x, 0, dev).start()

    def z2(self, h):
        x = self.p.x
        self.cp(0, h, x, 0, self.up).wait_recv()
        self.cp(1, h, x, 1, self.up).start()
        self.cp(2, h, x, 1, self.right).start()
        self.cp(3, h, x, 1, self.left).start()

    def z3(self, h):
        x = self.p.x
        self.cp(1, h, x, 1, self.up).wait_recv()
        for what, k, dev in ((4, self.kr, self.right), (5, self.kl, self.left)):
            @pl.when(k == 2)
            def _():
                self.cp(what, h, x, 2, dev).start()

    def far(self, h):
        self.cp(2, h, self.xl, 1, self.right).wait_recv()
        self.cp(3, h, self.xr, 1, self.left).wait_recv()
        self.cp(4, h, self.xl, kind(self.xl, self.p.x), self.right).wait_recv()
        self.cp(5, h, self.xr, kind(self.xr, self.p.x), self.left).wait_recv()
        self.cp(6, h, self.xl, self.fr, self.right).start()
        self.cp(7, h, self.xr, self.fl, self.left).start()

    def end(self, h):
        xf = (self.p.x + 2) % 4
        one = kind(xf, self.p.x)
        self.cp(6, h, xf, jnp.where(xf < 2, one, 1), self.right).wait_recv()
        self.cp(7, h, xf, jnp.where(xf < 2, 1, one), self.left).wait_recv()

    def sends(self, h):
        x = self.p.x
        for what in range(8):
            self.cp(what, h, x, 0, self.right).wait_send()


def rope(field, cosine, sine, sign):
    out = []
    for head in range(KVH):
        part = field[:, head * HD : (head + 1) * HD]
        out.append(part * cosine + sign * (pltpu.roll(part, HD // 2, 1) * sine))
    return jnp.concatenate(out, axis=1)


def forward_kernel(hid, w, v, cosine, sine, kb_o, vb_o, ha_o, ha, rel, wb, kb, vb, pcs, pcr, po, pys, pyr, send, recv, loc):
    p = Place()
    lo, y, c, zh, x, j = p.lo, p.y, p.c, p.zh, p.x, p.j
    copies = Copies(send, recv)
    yr, yl, yf = (y + 1) % 4, (y + 3) % 4, (y + 2) % 4
    mate = p.at(c=1 - c)
    xs = [(x + d) % 4 for d in (1, 3, 2)]
    peers = [mate]
    for yy in (yr, yl, yf):
        peers += [p.at(y=yy, c=0), p.at(y=yy, c=1)]
    peers += [p.at(x=xx) for xx in xs]
    peers += [p.z_next(), p.z_prev(), p.at(zh=(zh + 1) % 4), p.at(zh=(zh + 3) % 4)]

    part = x // 2 == c
    b = x % 2
    r = (zh - y + 4) % 4
    root = r == 0
    upward = ((r == 0) & (lo == 1)) | (r == 1) | ((r == 2) & (lo == 0))
    last = r == 2
    forward = part & jnp.logical_not(last)
    takes = part & jnp.logical_not(root)

    local_w = pltpu.make_async_copy(w, wb.at[b], loc.at[0])
    local_v = pltpu.make_async_copy(v, vb.at[x, 0], loc.at[1])
    local_h = pltpu.make_async_copy(hid.at[:, pl.ds(pl.multiple_of(j * 768, 128), 768)], ha.at[j], loc.at[2])

    @pl.when(part & root)
    def _():
        local_w.start()

    local_v.start()
    local_h.start()
    greet(peers)

    def piece(yy, cc):
        return hid.at[:, pl.ds(pl.multiple_of((2 * yy + cc) * 768, 128), 768)]

    i_rel = copies.new(2)
    rel_r = copies.make(piece(yf, 0), rel.at[0], i_rel, p.at(y=yr))
    rel_l = copies.make(piece(yf, 1), rel.at[1], i_rel + 1, p.at(y=yl))
    rel_r.start()
    rel_l.start()
    i_dir = copies.new(5)
    direct = []
    for n, (yy, cc) in enumerate(((yr, c), (yl, c), (yr, 1 - c), (yl, 1 - c), (y, 1 - c))):
        direct.append(copies.make(piece(yy, cc), ha.at[j], i_dir + n, p.at(y=yy, c=cc)))
    i_fw = copies.new(4)

    i_wz = copies.new(NQ)
    i_wx = copies.new(3 * NQ)
    rows = 384 // NQ

    def wz(q, dev):
        ref = wb.at[b, pl.ds(q * rows, rows), :]
        return copies.make(ref, ref, i_wz + q, dev)

    def wz_start(q):
        @pl.when(forward & upward)
        def _():
            wz(q, p.z_next()).start()

        @pl.when(forward & jnp.logical_not(upward))
        def _():
            wz(q, p.z_prev()).start()

    def wx(q, n, slot, dev):
        ref = wb.at[slot, pl.ds(q * rows, rows), :]
        return copies.make(ref, ref, i_wx + 3 * q + n, dev)

    def wx_start(q):
        @pl.when(part)
        def _():
            for n in (2, 0, 1):
                wx(q, n, b, p.at(x=xs[n])).start()

    @pl.when(part & root)
    def _():
        local_w.wait()

    for q in range(NQ):
        @pl.when(part & root)
        def _():
            wz_start(q)

    for d in direct:
        d.start()
    local_v.wait()
    gv = Gather(p, copies, vb)
    gv.z1(0)
    gv.z1(1)

    def w_step(q):
        @pl.when(takes)
        def _():
            wz(q, p.z_next()).wait_recv()
            wz_start(q)

        wx_start(q)

    w_step(0)
    w_step(1)
    rel_r.wait_recv()
    fw_r = copies.make(rel.at[0], ha.at[2 * yl + c], i_fw + c, p.at(y=yr, c=0))
    fw_r.start()
    rel_l.wait_recv()
    fw_l = copies.make(rel.at[1], ha.at[2 * yr + c], i_fw + 2 + c, p.at(y=yl, c=1))
    fw_l.start()
    w_step(2)
    w_step(3)
    gv.z2(0)
    gv.z2(1)

    for q in range(NQ):
        for slot in range(2):
            src = 2 * c + slot
            away = (src - x + 4) % 4
            for n, dist in ((0, 3), (1, 1), (2, 2)):
                @pl.when(away == dist)
                def _():
                    wx(q, n, slot, p.at(x=xs[n])).wait_recv()

    local_h.wait()
    for d in direct:
        d.wait_recv()
    for n in range(2):
        copies.make(rel.at[n], ha.at[2 * yf + n], i_fw + 2 * c + n, p.at(y=yr)).wait_recv()

    weights = wb[...].reshape(768, 512)

    i_pc = copies.new(4)
    order = (yf, yr, yl, y)
    to_mate = []
    for n, yy in enumerate(order):
        pcs[n] = jnp.dot(ha[2 * yy + 1 - c], weights, preferred_element_type=F32).astype(BF)
        cp = copies.make(pcs.at[n], pcr.at[n], i_pc + n, mate)
        cp.start()
        to_mate.append(cp)
    i_py = copies.new(3)
    to_y = []
    for n, yy in enumerate(order):
        own = jnp.dot(ha[2 * yy + c], weights, preferred_element_type=F32)
        to_mate[n].wait_recv()
        total = own + pcr[n].astype(F32)
        if n < 3:
            pys[n] = total.astype(BF)
            cp = copies.make(pys.at[n], pyr.at[n], i_py + n, p.at(y=yy))
            cp.start()
            to_y.append(cp)
        else:
            po[...] = total
    for cp in to_y:
        cp.wait_recv()
    raw = po[...] + pyr[0].astype(F32) + pyr[1].astype(F32) + pyr[2].astype(F32)
    kb[x, 0] = rope(raw, cosine[...], sine[...], 1.0).astype(BF)

    gk = Gather(p, copies, kb)
    both = (0, 1)
    for h in both:
        gk.z1(h)
    for h in both:
        gv.z3(h)
    for h in both:
        gk.z2(h)
    for h in both:
        gv.far(h)
    for h in both:
        gk.z3(h)
    for h in both:
        gk.far(h)
    for h in both:
        gv.end(h)
    ha_out = pltpu.make_async_copy(ha, ha_o, loc.at[3])
    vb_out = pltpu.make_async_copy(vb, vb_o, loc.at[4])
    ha_out.start()
    vb_out.start()
    for h in both:
        gk.end(h)
    kb_out = pltpu.make_async_copy(kb, kb_o, loc.at[5])
    kb_out.start()

    rel_r.wait_send()
    rel_l.wait_send()
    for cp in direct + [fw_r, fw_l] + to_mate + to_y:
        cp.wait_send()
    for q in range(NQ):
        @pl.when(forward)
        def _():
            wz(q, p.z_next()).wait_send()

        @pl.when(part)
        def _():
            for n in range(3):
                wx(q, n, b, p.at(x=xs[n])).wait_send()
    for h in both:
        gv.sends(h)
        gk.sends(h)
    ha_out.wait()
    vb_out.wait()
    kb_out.wait()


def attention_kernel(q, do, k, v, qd, kd, out, dq, dk, dv, probs, ds_all, bias, kc, vc, qs, dos):
    x = lax.axis_index("seq") % 4
    rows = q.shape[0]
    keys = kd.shape[1]
    scale = 1.0 / math.sqrt(HD)

    @pl.when(pl.program_id(0) == 0)
    def _():
        row = lax.broadcasted_iota(jnp.int32, (rows, keys), 0)
        col = lax.broadcasted_iota(jnp.int32, (rows, keys), 1)
        seen = (qd[...] == kd[...]) & (col - (keys - rows) <= row)
        bias[...] = jnp.where(seen, 0.0, -1e30)

    for n in range(9):
        xs, kk = (x + n) % 4, 2 - (x + n) // 4
        kc[n * rows : (n + 1) * rows] = k[xs, kk]
        vc[n * rows : (n + 1) * rows] = v[xs, kk]
    nt = (((1,), (1,)), ((), ()))
    tn = (((0,), (0,)), ((), ()))
    for h in range(GROUP):
        at = slice(h * HD, (h + 1) * HD)
        to = slice(h * rows, (h + 1) * rows)
        qh = q[:, at]
        doh = do[:, at]
        qs[to] = qh
        dos[to] = doh
        s = lax.dot_general(qh, kc[...], nt, preferred_element_type=F32)
        w = jnp.exp2(s * (scale * math.log2(math.e)) + bias[...])
        total = jnp.sum(w, axis=1, keepdims=True)
        inverse = 1.0 / total
        mixed = jnp.dot(w.astype(BF), vc[...], preferred_element_type=F32)
        attended = (mixed * inverse).astype(BF)
        out[:, at] = attended
        delta = jnp.sum(doh.astype(F32) * attended.astype(F32), axis=1, keepdims=True)
        prob = w * inverse
        probs[to] = prob.astype(BF)
        dprob = lax.dot_general(doh, vc[...], nt, preferred_element_type=F32)
        ds = (prob * (dprob - delta)).astype(BF)
        ds_all[to] = ds
        dq[:, at] = (jnp.dot(ds, kc[...], preferred_element_type=F32) * scale).astype(BF)
    dvc = lax.dot_general(probs[...], dos[...], tn, preferred_element_type=F32).astype(BF)
    dkc = (lax.dot_general(ds_all[...], qs[...], tn, preferred_element_type=F32) * scale).astype(BF)
    for n in range(9):
        xs, kk = (x + n) % 4, 2 - (x + n) // 4
        dk[xs, kk] = dkc[n * rows : (n + 1) * rows]
        dv[xs, kk] = dvc[n * rows : (n + 1) * rows]


class Scatter:
    def __init__(self, place, copies, buf, rn, rz, zs, acc):
        self.p, self.copies, self.buf = place, copies, buf
        self.rn, self.rz, self.zs, self.acc = rn, rz, zs, acc
        p = place
        x = p.x
        self.xl, self.xr, self.xf = (x + 3) % 4, (x + 1) % 4, (x + 2) % 4
        self.left, self.right = p.at(x=self.xl), p.at(x=self.xr)
        self.down = p.at(zh=(p.zh + 3) % 4)
        self.base = copies.new(16)

    def cp(self, what, h, src, dst, device):
        at = pl.ds(256 * h, 256)
        return self.copies.make(src.at[:, at], dst.at[:, at], self.base + 2 * what + h, device)

    def start(self, h):
        x, xl, xr, xf = self.p.x, self.xl, self.xr, self.xf
        buf, rn = self.buf, self.rn
        one = kind(xf, x)
        self.cp(0, h, buf.at[xf, jnp.where(xf < 2, one, 1)], rn.at[0], self.left).start()
        self.cp(1, h, buf.at[xf, jnp.where(xf < 2, 1, one)], rn.at[1], self.right).start()
        self.cp(2, h, buf.at[xl, jnp.where(xl < 2, 1, kind(xl, x))], rn.at[2], self.left).start()
        self.cp(3, h, buf.at[xr, jnp.where(xr < 2, kind(xr, x), 1)], rn.at[3], self.right).start()

    def add(self, h):
        x, xl, xr = self.p.x, self.xl, self.xr
        buf, rn = self.buf, self.rn
        at = pl.ds(256 * h, 256)
        for what, target, k, dev in (
            (0, xl, jnp.where(xl < 2, kind(xl, x), 1), self.left),
            (1, xr, jnp.where(xr < 2, 1, kind(xr, x)), self.right),
        ):
            self.cp(what, h, rn.at[what], rn.at[what], dev).wait_recv()
            both = buf[target, k, :, at].astype(F32) + rn[what, :, at].astype(F32)
            self.zs[what, :, at] = both.astype(BF)
            self.cp(4 + what, h, self.zs.at[what], rn.at[4 + what], dev).start()

    def own(self, h):
        x, xl, xr = self.p.x, self.xl, self.xr
        at = pl.ds(256 * h, 256)
        for k in range(3):
            self.acc[k, :, at] = self.buf[x, k, :, at].astype(F32)
        for what, k in (
            (2, jnp.where(x < 2, 1, kind(x, xr))),
            (3, jnp.where(x < 2, kind(x, xl), 1)),
            (4, jnp.where(x < 2, kind(x, xr), 1)),
            (5, jnp.where(x < 2, 1, kind(x, xl))),
        ):
            self.cp(what, h, self.rn.at[what], self.rn.at[what], self.left).wait_recv()
            self.acc[k, :, at] += self.rn[what, :, at].astype(F32)
        self.zs[2, :, at] = self.acc[2, :, at].astype(BF)
        self.cp(6, h, self.zs.at[2], self.rz.at[0], self.down).start()

    def z2(self, h):
        at = pl.ds(256 * h, 256)
        self.cp(6, h, self.rz.at[0], self.rz.at[0], self.down).wait_recv()
        self.zs[3, :, at] = (self.acc[1, :, at] + self.rz[0, :, at].astype(F32)).astype(BF)
        self.cp(7, h, self.zs.at[3], self.rz.at[1], self.down).start()

    def end(self, h):
        at = pl.ds(256 * h, 256)
        self.cp(7, h, self.rz.at[1], self.rz.at[1], self.down).wait_recv()
        self.acc[0, :, at] += self.rz[1, :, at].astype(F32)

    def sends(self, h):
        for what in range(8):
            self.cp(what, h, self.rn.at[0], self.rn.at[0], self.left).wait_send()


def backward_kernel(
    dkb, dvb, ha, cosine, sine, gv_o, gw_o,
    krn, krz, kzs, kacc, vrn, vrz, vzs, vacc, kga, wg, wx1, wx2, wzr, wsum, wfin, send, recv,
):
    p = Place()
    lo, y, c, zh, x, j = p.lo, p.y, p.c, p.zh, p.x, p.j
    copies = Copies(send, recv)
    yr, yl, yf = (y + 1) % 4, (y + 3) % 4, (y + 2) % 4
    xl, xr = (x + 3) % 4, (x + 1) % 4
    mate = p.at(c=1 - c)
    up_z, down_z = p.z_next(), p.z_prev()
    greet(
        [mate, p.at(y=yr), p.at(y=yl), p.at(y=yf), p.at(x=xl), p.at(x=xr), up_z, down_z]
        + [p.at(zh=(zh + 1) % 4), p.at(zh=(zh + 3) % 4)]
    )
    sk = Scatter(p, copies, dkb, krn, krz, kzs, kacc)
    sv = Scatter(p, copies, dvb, vrn, vrz, vzs, vacc)
    both = (0, 1)
    for h in both:
        sk.start(h)
    for h in both:
        sk.add(h)
    for h in both:
        sk.own(h)
    for h in both:
        sv.start(h)
    for h in both:
        sk.z2(h)
    for h in both:
        sv.add(h)
    for h in both:
        sk.end(h)

    kga[j] = rope(kacc[0], cosine[...], sine[...], -1.0).astype(BF)
    i_ky = copies.new(4)
    i_kc = copies.new(3)
    gives = []
    for n, yy in enumerate((yf, yr, yl)):
        gives.append(copies.make(kga.at[j], kga.at[j], i_ky + n, p.at(y=yy)))
    gives.append(copies.make(kga.at[j], kga.at[j], i_ky + 3, mate))
    for cp in gives:
        cp.start()
    passes = []
    for n, yy in ((1, yl), (2, yr), (0, yf)):
        gives[n].wait_recv()
        ref = kga.at[2 * yy + c]
        cp = copies.make(ref, ref, i_kc + n, mate)
        cp.start()
        passes.append(cp)
    gives[3].wait_recv()
    for h in both:
        sv.own(h)
    for cp in passes:
        cp.wait_recv()

    tn = (((0,), (0,)), ((), ()))
    tokens = kga[...].reshape(1024, 512)
    rows = 384 // NQ
    u = (x - 2 * c + 4) % 4
    given = jnp.where((u == 0) | (u == 3), 1, 0)
    kept = 1 - given
    even = u % 2 == 0
    ends = u < 2
    r = (zh - y + 4) % 4
    root = r == 0
    upward = ((r == 0) & (lo == 1)) | (r == 1) | ((r == 2) & (lo == 0))
    i_x1 = copies.new(NQ)
    i_x2 = copies.new(NQ)
    i_z = copies.new(NQ)
    i_l = copies.new(NQ)
    i_y = copies.new(3 * NQ)
    i_c = copies.new(NQ)
    sl = [pl.ds(q * rows, rows) for q in range(NQ)]

    def x1(q, dev):
        return copies.make(wg.at[given, sl[q], :], wx1.at[sl[q], :], i_x1 + q, dev)

    def x2(q, dev):
        return copies.make(wsum.at[sl[q], :], wx2.at[sl[q], :], i_x2 + q, dev)

    def zc(q, dev):
        return copies.make(wsum.at[sl[q], :], wzr.at[0, sl[q], :], i_z + q, dev)

    def lc(q):
        return copies.make(wsum.at[sl[q], :], wzr.at[1, sl[q], :], i_l + q, p.at(lo=1 - lo))

    def yc(q, n, yy):
        return copies.make(wfin.at[sl[q], :], wfin.at[sl[q], :], i_y + 3 * q + n, p.at(y=yy))

    def cc(q):
        return copies.make(wfin.at[sl[q], :], wfin.at[sl[q], :], i_c + q, mate)

    wide = ha[...].reshape(1024, 768)
    wg[...] = lax.dot_general(wide, tokens, tn, preferred_element_type=F32).reshape(2, 384, 512).astype(BF)
    for q in range(NQ):
        @pl.when(even)
        def _():
            x1(q, p.at(x=xr)).start()

        @pl.when(jnp.logical_not(even))
        def _():
            x1(q, p.at(x=xl)).start()

    for q in range(NQ):
        x1(q, p.at(x=xr)).wait_recv()
        wsum[sl[q], :] = (wg[kept, sl[q], :].astype(F32) + wx1[sl[q], :].astype(F32)).astype(BF)

        @pl.when(u == 2)
        def _():
            x2(q, p.at(x=xl)).start()

        @pl.when(u == 3)
        def _():
            x2(q, p.at(x=xr)).start()

    for h in both:
        sv.z2(h)

    for q in range(NQ):
        @pl.when(ends)
        def _():
            x2(q, p.at(x=xr)).wait_recv()
            total = wsum[sl[q], :].astype(F32) + wx2[sl[q], :].astype(F32)

            @pl.when(r == 2)
            def _():
                wsum[sl[q], :] = total.astype(BF)

            @pl.when(r != 2)
            def _():
                zc(q, up_z).wait_recv()
                wsum[sl[q], :] = (total + wzr[0, sl[q], :].astype(F32)).astype(BF)

            @pl.when(jnp.logical_not(root) & upward)
            def _():
                zc(q, down_z).start()

            @pl.when(jnp.logical_not(root) & jnp.logical_not(upward))
            def _():
                zc(q, up_z).start()

            @pl.when(root)
            def _():
                lc(q).start()

    for q in range(NQ):
        @pl.when(ends & root)
        def _():
            lc(q).wait_recv()
            total = wsum[sl[q], :].astype(F32) + wzr[1, sl[q], :].astype(F32)
            wfin[sl[q], :] = (total * (1.0 / 16.0)).astype(BF)
            for n, yy in enumerate((yf, yr, yl)):
                yc(q, n, yy).start()
            cc(q).start()

    away = (zh - y + 4) % 4
    for q in range(NQ):
        @pl.when(ends & jnp.logical_not(root))
        def _():
            for n, dist in ((0, 2), (1, 3), (2, 1)):
                @pl.when(away == dist)
                def _():
                    yc(q, n, yf).wait_recv()
            cc(q).start()

        @pl.when(jnp.logical_not(ends))
        def _():
            cc(q).wait_recv()

        gw_o[sl[q], :] = wfin[sl[q], :].astype(F32)

    for h in both:
        sv.end(h)
    gv_o[...] = vacc[0].astype(BF)

    for cp in gives + passes:
        cp.wait_send()
    for q in range(NQ):
        x1(q, p.at(x=xr)).wait_send()

        @pl.when(jnp.logical_not(ends))
        def _():
            x2(q, p.at(x=xr)).wait_send()

        @pl.when(ends)
        def _():
            cc(q).wait_send()

            @pl.when(root)
            def _():
                lc(q).wait_send()
                for n, yy in enumerate((yf, yr, yl)):
                    yc(q, n, yy).wait_send()

            @pl.when(jnp.logical_not(root))
            def _():
                zc(q, up_z).wait_send()
    for h in both:
        sk.sends(h)
        sv.sends(h)


def vmem():
    return pl.BlockSpec(memory_space=pltpu.VMEM)


def local(inputs, queries, values, key_weight, doc_ids, grad_out):
    rows = inputs.shape[1]
    width = 512
    sq = lax.axis_index("seq")
    positions = sq * rows + jnp.arange(rows)
    half = HD // 2
    freqs = ROPE_BASE ** (-(jnp.arange(half).astype(F32) * 2.0 / HD))
    angles = positions.astype(F32)[:, None] * freqs[None, :]
    cos, sin = jnp.cos(angles), jnp.sin(angles)
    cosine = jnp.concatenate([cos, cos], axis=1)
    sine = jnp.concatenate([-sin, sin], axis=1)

    any_spec = pl.BlockSpec(memory_space=pl.ANY)
    dma = pltpu.SemaphoreType.DMA
    blocks = (4, 3, rows, width)
    kb, vb, ha = pl.pallas_call(
        forward_kernel,
        out_shape=(
            jax.ShapeDtypeStruct(blocks, BF),
            jax.ShapeDtypeStruct(blocks, BF),
            jax.ShapeDtypeStruct((8, rows, 768), BF),
        ),
        in_specs=[any_spec, any_spec, any_spec, vmem(), vmem()],
        out_specs=(any_spec, any_spec, any_spec),
        scratch_shapes=[
            pltpu.VMEM((8, rows, 768), BF),
            pltpu.VMEM((2, rows, 768), BF),
            pltpu.VMEM((2, 384, width), BF),
            pltpu.VMEM(blocks, BF),
            pltpu.VMEM(blocks, BF),
            pltpu.VMEM((4, rows, width), BF),
            pltpu.VMEM((4, rows, width), BF),
            pltpu.VMEM((rows, width), F32),
            pltpu.VMEM((3, rows, width), BF),
            pltpu.VMEM((3, rows, width), BF),
            dma((96,)),
            dma((96,)),
            dma((6,)),
        ],
        compiler_params=pltpu.CompilerParams(
            collective_id=0, has_side_effects=True, vmem_limit_bytes=VMEM_LIMIT
        ),
        name="forward_exchange",
    )(inputs[0], key_weight, values[0], cosine, sine)

    keys = 9 * rows
    padded = jnp.concatenate([jnp.full((8 * rows,), -1, jnp.int32), doc_ids[0]])
    key_docs = lax.dynamic_slice_in_dim(padded, sq * rows, keys, 0)
    query_docs = key_docs[8 * rows :]
    head = GROUP * HD
    attn, dq, dkb, dvb = pl.pallas_call(
        attention_kernel,
        grid=(KVH,),
        out_shape=(
            jax.ShapeDtypeStruct((rows, QH * HD), BF),
            jax.ShapeDtypeStruct((rows, QH * HD), BF),
            jax.ShapeDtypeStruct(blocks, BF),
            jax.ShapeDtypeStruct(blocks, BF),
        ),
        in_specs=[
            pl.BlockSpec((rows, head), lambda g: (0, g)),
            pl.BlockSpec((rows, head), lambda g: (0, g)),
            pl.BlockSpec((4, 3, rows, HD), lambda g: (0, 0, 0, g)),
            pl.BlockSpec((4, 3, rows, HD), lambda g: (0, 0, 0, g)),
            pl.BlockSpec((rows, 1), lambda g: (0, 0)),
            pl.BlockSpec((1, keys), lambda g: (0, 0)),
        ],
        out_specs=(
            pl.BlockSpec((rows, head), lambda g: (0, g)),
            pl.BlockSpec((rows, head), lambda g: (0, g)),
            pl.BlockSpec((4, 3, rows, HD), lambda g: (0, 0, 0, g)),
            pl.BlockSpec((4, 3, rows, HD), lambda g: (0, 0, 0, g)),
        ),
        scratch_shapes=[
            pltpu.VMEM((GROUP * rows, keys), BF),
            pltpu.VMEM((GROUP * rows, keys), BF),
            pltpu.VMEM((rows, keys), F32),
            pltpu.VMEM((keys, HD), BF),
            pltpu.VMEM((keys, HD), BF),
            pltpu.VMEM((GROUP * rows, HD), BF),
            pltpu.VMEM((GROUP * rows, HD), BF),
        ],
        compiler_params=pltpu.CompilerParams(vmem_limit_bytes=VMEM_LIMIT),
        name="attention",
    )(queries[0], grad_out[0], kb, vb, query_docs[:, None], key_docs[None, :])

    block = (rows, width)
    per_sum = [
        pltpu.VMEM((6,) + block, BF),
        pltpu.VMEM((2,) + block, BF),
        pltpu.VMEM((4,) + block, BF),
        pltpu.VMEM((3,) + block, F32),
    ]
    grad_values, weight_grad = pl.pallas_call(
        backward_kernel,
        out_shape=(
            jax.ShapeDtypeStruct(block, BF),
            jax.ShapeDtypeStruct((384, width), F32),
        ),
        in_specs=[vmem()] * 5,
        out_specs=(vmem(), vmem()),
        scratch_shapes=per_sum
        + per_sum
        + [
            pltpu.VMEM((8,) + block, BF),
            pltpu.VMEM((2, 384, width), BF),
            pltpu.VMEM((384, width), BF),
            pltpu.VMEM((384, width), BF),
            pltpu.VMEM((2, 384, width), BF),
            pltpu.VMEM((384, width), BF),
            pltpu.VMEM((384, width), BF),
            dma((80,)),
            dma((80,)),
        ],
        compiler_params=pltpu.CompilerParams(
            collective_id=1, has_side_effects=True, vmem_limit_bytes=VMEM_LIMIT
        ),
        name="backward_exchange",
    )(dkb, dvb, ha, cosine, sine)
    return attn[None], dq[None], grad_values[None], weight_grad


def solution(mesh):
    in_specs = (
        P("dp", "seq", None),
        P("dp", "seq", None),
        P("dp", "seq", None),
        P("seq", None),
        P("dp", None),
        P("dp", "seq", None),
    )
    out_specs = (P("dp", "seq", None), P("dp", "seq", None), P("dp", "seq", None), P("seq", None))
    return jax.shard_map(local, mesh=mesh, in_specs=in_specs, out_specs=out_specs, check_vma=False)
```

```python
import math

import jax
import jax.numpy as jnp
import numpy as np
from jax import lax
from jax.experimental import pallas as pl
from jax.experimental.pallas import tpu as pltpu
from jax.sharding import PartitionSpec as P

QH = 24
KVH = 4
HD = 128
GROUP = QH // KVH
ROPE_BASE = 1000000.0
MESH = pl.DeviceIdType.MESH
BF = jnp.bfloat16
F32 = jnp.float32
NQ = 4
SENDS = 21
RECVS = 78
VMEM_LIMIT = 56 * 1024 * 1024


class Place:
    def __init__(self):
        dp = lax.axis_index("dp")
        sq = lax.axis_index("seq")
        self.lo = dp // 8
        self.y = (dp // 2) % 4
        self.c = dp % 2
        self.zh = sq // 4
        self.x = sq % 4
        self.j = dp % 8

    def at(self, lo=None, y=None, c=None, zh=None, x=None):
        lo = self.lo if lo is None else lo
        y = self.y if y is None else y
        c = self.c if c is None else c
        zh = self.zh if zh is None else zh
        x = self.x if x is None else x
        return (lo * 8 + y * 2 + c, zh * 4 + x)

    def z_next(self):
        return self.at(lo=1 - self.lo, zh=(self.zh + self.lo) % 4)

    def z_prev(self):
        return self.at(lo=1 - self.lo, zh=(self.zh + 3 + self.lo) % 4)


class Copies:
    def __init__(self, send, recv, other):
        self.send, self.recv, self.other = send, recv, other
        self.sends = self.recvs = 0

    def new_send(self, number=1):
        self.sends += number
        return self.sends - number

    def new_recv(self, number=1):
        self.recvs += number
        return self.recvs - number

    def make(self, src, dst, send, recv, device):
        return pltpu.make_async_remote_copy(
            src_ref=src,
            dst_ref=dst,
            send_sem=self.send.at[send],
            recv_sem=self.recv.at[recv],
            device_id=device,
            device_id_type=MESH,
        )

    def sent(self, ref, send):
        self.make(ref, ref, send, 0, self.other).wait_send()

    def got(self, ref, recv):
        self.make(ref, ref, 0, recv, self.other).wait_recv()


def greet(devices):
    barrier = pltpu.get_barrier_semaphore()
    for device in devices:
        pl.semaphore_signal(barrier, inc=1, device_id=device, device_id_type=MESH)
    pl.semaphore_wait(barrier, len(devices))


def kind(source, reader):
    return jnp.where(reader > source, 0, 2)


class Gather:
    def __init__(self, place, copies, buf):
        self.p, self.copies, self.buf = place, copies, buf
        self.out = copies.new_send()
        self.base = copies.new_recv(3 * KVH)

    def cp(self, what, g, k, to, device):
        x = self.p.x
        index = self.base + KVH * what + g
        self.copies.make(self.buf.at[g, x, k], self.buf.at[g, x, to], self.out, index, device).start()

    def across(self, g, k):
        p = self.p
        for d in (2, 1, 3):
            to = (p.x + d) % 4
            if k == 1:
                self.cp(2, g, 1, 1, p.at(x=to))
            else:
                @pl.when(kind(p.x, to) == k)
                def _():
                    self.cp(2, g, k, k, p.at(x=to))

    def start(self, g):
        p = self.p
        self.cp(0, g, 0, 1, p.at(zh=(p.zh + 1) % 4))
        self.cp(1, g, 0, 2, p.at(zh=(p.zh + 2) % 4))
        self.across(g, 0)

    def pass_on(self, g):
        for what in (0, 1):
            self.copies.got(self.buf.at[g, self.p.x, what + 1], self.base + KVH * what + g)
            self.across(g, what + 1)

    def end(self, g):
        self.copies.got(self.buf.at[g, 0:2], self.base + 2 * KVH + g)

    def sends(self):
        self.copies.sent(self.buf.at[:, :, 0:2], self.out)


class Scatter:
    def __init__(self, place, copies, buf, rn, rz, zs, acc):
        self.p, self.copies, self.buf = place, copies, buf
        self.rn, self.rz, self.zs, self.acc = rn, rz, zs, acc
        self.out = copies.new_send(2)
        self.base = copies.new_recv(2 * KVH)

    def start(self, g):
        p = self.p
        for d in (2, 1, 3):
            to = (p.x + d) % 4
            for slot, k in ((d - 1, kind(to, p.x)), (2 + d, 1)):
                self.copies.make(
                    self.buf.at[g, to, k], self.rn.at[g, slot], self.out, self.base + g, p.at(x=to)
                ).start()

    def across(self, g):
        p = self.p
        acc = self.acc
        self.copies.got(self.rn.at[g], self.base + g)
        for k in range(3):
            acc[g, k] = self.buf[g, p.x, k].astype(F32)
        for d in (1, 3, 2):
            k = kind(p.x, (p.x + 4 - d) % 4)
            acc[g, k] += self.rn[g, d - 1].astype(F32)
            acc[g, 1] += self.rn[g, 2 + d].astype(F32)
        for n, back in ((1, 2), (0, 3)):
            self.zs[g, n] = acc[g, n + 1].astype(BF)
            self.copies.make(
                self.zs.at[g, n], self.rz.at[g, n], self.out + 1, self.base + KVH + g, p.at(zh=(p.zh + back) % 4)
            ).start()

    def end(self, g):
        self.copies.got(self.rz.at[g], self.base + KVH + g)
        return self.acc[g, 0] + self.rz[g, 0].astype(F32) + self.rz[g, 1].astype(F32)

    def sends(self):
        self.copies.sent(self.rn, self.out)
        self.copies.sent(self.rz, self.out + 1)


def spread(table):
    lane = lax.broadcasted_iota(jnp.int32, table.shape, 1)
    turned = pltpu.roll(table, HD // 2, 1)
    return jnp.where(lane < HD // 2, table, turned), jnp.where(lane < HD // 2, -turned, table)


def rope(part, cosine, sine, sign):
    return part * cosine + sign * (pltpu.roll(part, HD // 2, 1) * sine)


def whole_kernel(
    hid, w, v, q_in, do_in, docs, table,
    out_o, dq_o, gv_o, gw_o,
    q, do, out, dq,
    ha, hat, wb, kb, vb, po, pcs, pcr, pys, pyr, tab,
    probs, ds_all, bias, kc, vc, qs, dos,
    dkb, dvb, krn, vrn, krz, vrz, kzs, vzs, kacc, vacc,
    kga, wg, wxr, wsum, wzr, wlo, wlr, wfin,
    send, recv, loc,
):
    p = Place()
    lo, y, c, zh, x, j = p.lo, p.y, p.c, p.zh, p.x, p.j
    yr, yl, yf = (y + 1) % 4, (y + 3) % 4, (y + 2) % 4
    mate = p.at(c=1 - c)
    copies = Copies(send, recv, mate)
    up_z, down_z = p.z_next(), p.z_prev()
    xs = [(x + d) % 4 for d in (1, 3, 2)]
    peers = [mate]
    for yy in (yr, yl, yf):
        peers += [p.at(y=yy, c=0), p.at(y=yy, c=1)]
    peers += [p.at(x=xx) for xx in xs]
    for d in (1, 2, 3):
        peers += [p.at(zh=(zh + d) % 4), p.at(zh=(zh + d) % 4, lo=1 - lo)]
    peers.append(p.at(lo=1 - lo))
    rows = HD
    scale = 1.0 / math.sqrt(HD)

    part = x // 2 == c
    b = x % 2
    r = (zh - y + 4) % 4
    root = r == 0
    upward = ((r == 0) & (lo == 1)) | (r == 1) | ((r == 2) & (lo == 0))
    forward = part & (r != 2)
    takes = part & jnp.logical_not(root)

    local_w = pltpu.make_async_copy(w, wb.at[b], loc.at[0])
    local_h = pltpu.make_async_copy(hid.at[:, pl.ds(pl.multiple_of(j * 768, 128), 768)], ha.at[y, c], loc.at[1])
    place = pl.multiple_of((zh * 4 + x) * rows, rows)
    local_t = pltpu.make_async_copy(table.at[pl.ds(place, rows), :], tab, loc.at[2])
    local_q = pltpu.make_async_copy(q_in, q, loc.at[3])
    local_do = pltpu.make_async_copy(do_in, do, loc.at[4])
    local_v = [
        pltpu.make_async_copy(v.at[:, g * HD : (g + 1) * HD], vb.at[g, x, 0], loc.at[5 + g]) for g in range(KVH)
    ]

    @pl.when(part & root)
    def _():
        local_w.start()

    local_h.start()
    for cp in local_v:
        cp.start()
    local_t.start()
    local_q.start()
    local_do.start()
    greet(peers)

    def piece(yy, cc):
        return hid.at[:, pl.ds(pl.multiple_of((2 * yy + cc) * 768, 128), 768)]

    s_wz, r_wz = copies.new_send(NQ), copies.new_recv(NQ)
    s_wx, r_wx = copies.new_send(), copies.new_recv()
    wrows = 384 // NQ

    def wpart(n):
        return wb.at[b, pl.ds(n * wrows, wrows), :]

    def w_start(n):
        ref = wpart(n)

        @pl.when(forward & upward)
        def _():
            copies.make(ref, ref, s_wz + n, r_wz + n, up_z).start()

        @pl.when(forward & jnp.logical_not(upward))
        def _():
            copies.make(ref, ref, s_wz + n, r_wz + n, down_z).start()

        @pl.when(part)
        def _():
            for m in (2, 0, 1):
                copies.make(ref, ref, s_wx, r_wx, p.at(x=xs[m])).start()

    @pl.when(part & root)
    def _():
        local_w.wait()
        w_start(0)
        w_start(1)

    seven = hat.at[0:672]
    s_dir, r_dir = copies.new_send(), copies.new_recv()
    for yy, cc in ((yf, c), (yf, 1 - c), (yr, c), (yr, 1 - c), (yl, c), (yl, 1 - c), (y, 1 - c)):
        copies.make(piece(yy, cc), ha.at[y, c], s_dir, r_dir, p.at(y=yy, c=cc)).start()

    @pl.when(part & root)
    def _():
        for n in range(2, NQ):
            copies.sent(wpart(n - 2), s_wz + n - 2)
            w_start(n)

    gv = Gather(p, copies, vb)
    gk = Gather(p, copies, kb)

    @pl.when(takes)
    def _():
        for n in range(NQ):
            copies.got(wpart(n), r_wz + n)
            w_start(n)

    for cp in local_v:
        cp.wait()
    gv.start(0)

    @pl.when(part)
    def _():
        copies.got(wb.at[0], r_wx)

    @pl.when(jnp.logical_not(part))
    def _():
        copies.got(wb, r_wx)

    gv.start(1)
    gv.start(2)
    gv.start(3)
    gv.pass_on(0)
    local_h.wait()
    local_t.wait()
    cosine, sine = spread(tab[...])
    s_pc, r_pc = copies.new_send(), copies.new_recv(2)
    s_py, r_py = copies.new_send(), copies.new_recv(2)
    copies.got(seven, r_dir)
    for half in range(2):
        weights = wb[:, :, half * 256 : (half + 1) * 256].reshape(768, 256)
        theirs = jnp.dot(ha[:, 1 - c].reshape(512, 768), weights, preferred_element_type=F32)
        pcs[half] = theirs.astype(BF).reshape(4, rows, 256)
        copies.make(pcs.at[half], pcr.at[half], s_pc, r_pc + half, mate).start()
        po[half] = jnp.dot(ha[:, c].reshape(512, 768), weights, preferred_element_type=F32).reshape(4, rows, 256)
    for half in range(2):
        copies.got(pcr.at[half], r_pc + half)
        for n, yy in enumerate((yf, yr, yl)):
            pys[half, n] = (po[half, yy] + pcr[half, yy].astype(F32)).astype(BF)
            copies.make(pys.at[half, n], pyr.at[half, n], s_py, r_py + half, p.at(y=yy)).start()

    def keys_of(half):
        total = po[half, y] + pcr[half, y].astype(F32)
        copies.got(pyr.at[half], r_py + half)
        for n in range(3):
            total = total + pyr[half, n].astype(F32)
        for n in range(2):
            kb[2 * half + n, x, 0] = rope(total[:, n * HD : (n + 1) * HD], cosine, sine, 1.0).astype(BF)

    gv.pass_on(1)
    gv.pass_on(2)
    keys_of(0)
    gk.start(0)
    keys_of(1)
    gk.start(1)
    gv.pass_on(3)

    position = zh * 4 + x
    own_docs = jnp.broadcast_to(docs[:, pl.ds(place, rows)], (rows, rows)).T
    row = lax.broadcasted_iota(jnp.int32, (rows, rows), 0)
    col = lax.broadcasted_iota(jnp.int32, (rows, rows), 1)
    for n in range(9):
        block = position - 8 + n
        start = pl.multiple_of(jnp.maximum(block, 0) * rows, rows)
        seen = own_docs == docs[:, pl.ds(start, rows)]
        if n == 8:
            seen = seen & (col <= row)
        column = jnp.where(seen, jnp.where(block >= 0, 0.0, -1e30), -1e30)
        bias[:rows, n * rows : (n + 1) * rows] = column
        bias[rows:, n * rows : (n + 1) * rows] = column
    gk.pass_on(0)
    gk.start(2)
    gk.pass_on(1)
    gk.start(3)
    hat[...] = ha[...].reshape(1024, 768).T
    local_q.wait()
    local_do.wait()

    sk = Scatter(p, copies, dkb, krn, krz, kzs, kacc)
    sv = Scatter(p, copies, dvb, vrn, vrz, vzs, vacc)
    s_ky, r_ky = copies.new_send(), copies.new_recv(KVH)
    s_kp, r_kp = copies.new_send(), copies.new_recv(KVH)

    def key_grad(g):
        cos1, sin1 = spread(tab[...])
        kga[g, j] = rope(sk.end(g), cos1, sin1, -1.0).astype(BF)
        ref = kga.at[g, j]
        for yy in (yf, yr, yl):
            copies.make(ref, ref, s_ky, r_ky + g, p.at(y=yy)).start()
        copies.make(ref, ref, s_kp, r_kp + g, mate).start()

    def key_pass(g):
        copies.got(kga.at[g, 0:3], r_ky + g)
        for yy in (yf, yr, yl):
            ref = kga.at[g, 2 * yy + c]
            copies.make(ref, ref, s_kp, r_kp + g, mate).start()

    nt = (((1,), (1,)), ((), ()))
    tn = (((0,), (0,)), ((), ()))

    u = (x - 2 * c + 4) % 4
    s_x, r_x = copies.new_send(), copies.new_recv(KVH)
    s_z, r_z = copies.new_send(), copies.new_recv(KVH)
    s_l, r_l = copies.new_send(), copies.new_recv(KVH)
    s_y, r_y = copies.new_send(), copies.new_recv(KVH)
    s_c, r_c = copies.new_send(), copies.new_recv(KVH)
    steps = jnp.where(upward, 2 * r + lo - 1, 2 * (4 - r) - lo)
    top = p.at(lo=jnp.where(upward, 1, 0), zh=y)

    def weight_grad(g):
        copies.got(kga.at[g, 0:4], r_kp + g)
        for t in range(2):
            wg[g, t] = jnp.dot(
                hat[t * 384 : (t + 1) * 384, :], kga[g].reshape(1024, HD), preferred_element_type=F32
            ).astype(BF)

            @pl.when(u != t)
            def _():
                d = (u - t + 3) % 4
                copies.make(wg.at[g, t], wxr.at[g, d], s_x, r_x + g, p.at(x=2 * c + t)).start()

    def x_sum(g):
        @pl.when(part)
        def _():
            total = wg[g, b].astype(F32)
            copies.got(wxr.at[g], r_x + g)
            for d in range(3):
                total = total + wxr[g, d].astype(F32)
            wsum[g] = total.astype(BF)

            @pl.when(jnp.logical_not(root))
            def _():
                copies.make(wsum.at[g], wzr.at[g, steps - 1], s_z, r_z + g, top).start()

    def z_sum(g):
        @pl.when(part & root)
        def _():
            total = wsum[g].astype(F32)
            copies.got(wzr.at[g], r_z + g)
            for d in range(3):
                total = total + wzr[g, d].astype(F32)
            wlo[g] = total.astype(BF)
            copies.make(wlo.at[g], wlr.at[g], s_l, r_l + g, p.at(lo=1 - lo)).start()

    def finish(g):
        @pl.when(part & root)
        def _():
            copies.got(wlr.at[g], r_l + g)
            total = wlo[g].astype(F32) + wlr[g].astype(F32)
            wfin[g] = (total * (1.0 / 16.0)).astype(BF)
            for yy in (yf, yr, yl):
                copies.make(wfin.at[g], wfin.at[g], s_y, r_y + g, p.at(y=yy)).start()
            copies.make(wfin.at[g], wfin.at[g], s_c, r_c + g, mate).start()

    def take(g):
        @pl.when(part & jnp.logical_not(root))
        def _():
            copies.got(wfin.at[g], r_y + g)
            copies.make(wfin.at[g], wfin.at[g], s_c, r_c + g, mate).start()

    def keep(g):
        @pl.when(jnp.logical_not(part))
        def _():
            copies.got(wfin.at[g], r_c + g)

        gw_o[:, g * HD : (g + 1) * HD] = wfin[g].astype(F32)

    def value_out(g):
        gv_o[:, g * HD : (g + 1) * HD] = sv.end(g).astype(BF)

    def ready(g):
        gk.end(g)
        gv.end(g)

    def away_copy(n, g):
        at = pl.ds(pl.multiple_of(g * (GROUP * HD), HD), GROUP * HD)
        src, dst = ((out, out_o), (dq, dq_o))[n]
        return pltpu.make_async_copy(src.at[:, at], dst.at[:, at], loc.at[9 + KVH * n + g])

    def head(g, carry):
        ready(g)
        for n in range(9):
            xx, kk = (x + n) % 4, 2 - (x + n) // 4
            kc[n * rows : (n + 1) * rows] = kb[g, xx, kk]
            vc[n * rows : (n + 1) * rows] = vb[g, xx, kk]

        def lanes(h):
            return pl.ds(pl.multiple_of(g * (GROUP * HD) + h * HD, HD), HD)

        for h in range(GROUP):
            qs[h * rows : (h + 1) * rows] = q[:, lanes(h)]
            dos[h * rows : (h + 1) * rows] = do[:, lanes(h)]
        for pair in range(GROUP // 2):
            to = slice(pair * 2 * rows, (pair + 1) * 2 * rows)
            s = lax.dot_general(qs[to], kc[...], nt, preferred_element_type=F32)
            wt = jnp.exp2(s * (scale * math.log2(math.e)) + bias[...])
            inverse = 1.0 / jnp.sum(wt, axis=1, keepdims=True)
            mixed = jnp.dot(wt.astype(BF), vc[...], preferred_element_type=F32)
            attended = (mixed * inverse).astype(BF)
            delta = jnp.sum(dos[to].astype(F32) * attended.astype(F32), axis=1, keepdims=True)
            prob = wt * inverse
            probs[to] = prob.astype(BF)
            dprob = lax.dot_general(dos[to], vc[...], nt, preferred_element_type=F32)
            ds = (prob * (dprob - delta)).astype(BF)
            ds_all[to] = ds
            dquery = (jnp.dot(ds, kc[...], preferred_element_type=F32) * scale).astype(BF)
            for n in range(2):
                out[:, lanes(2 * pair + n)] = attended[n * rows : (n + 1) * rows]
                dq[:, lanes(2 * pair + n)] = dquery[n * rows : (n + 1) * rows]
            if pair == 0:
                @pl.when(g == 0)
                def _():
                    gk.pass_on(2)

                @pl.when(g >= 2)
                def _():
                    sv.across(g - 2)

                @pl.when(g >= 3)
                def _():
                    weight_grad(g - 3)
            if pair == 1:
                @pl.when(g == 0)
                def _():
                    gk.pass_on(3)

                @pl.when(g >= 2)
                def _():
                    key_grad(g - 2)

                @pl.when(g >= 1)
                def _():
                    sk.across(g - 1)
        dkc = (lax.dot_general(ds_all[...], qs[...], tn, preferred_element_type=F32) * scale).astype(BF)
        for n in range(9):
            dkb[g, (x + n) % 4, 2 - (x + n) // 4] = dkc[n * rows : (n + 1) * rows]
        sk.start(g)
        dvc = lax.dot_general(probs[...], dos[...], tn, preferred_element_type=F32).astype(BF)
        for n in range(9):
            dvb[g, (x + n) % 4, 2 - (x + n) // 4] = dvc[n * rows : (n + 1) * rows]
        @pl.when(g < KVH - 1)
        def _():
            sv.start(g)

        away_copy(0, g).start()
        away_copy(1, g).start()

        @pl.when(g >= 2)
        def _():
            key_pass(g - 2)

        return carry

    lax.fori_loop(0, KVH, head, 0)

    x_sum(0)
    weight_grad(1)
    key_grad(2)
    sk.across(3)
    key_pass(2)
    x_sum(1)
    key_grad(3)
    sv.start(3)
    sv.across(2)
    weight_grad(2)
    key_pass(3)
    x_sum(2)
    z_sum(0)
    finish(0)
    weight_grad(3)
    sv.across(3)
    z_sum(1)
    finish(1)
    take(0)
    x_sum(3)
    z_sum(2)
    finish(2)
    take(1)
    keep(0)
    z_sum(3)
    take(2)
    finish(3)
    keep(1)
    keep(2)
    for g in range(KVH):
        value_out(g)
    take(3)
    keep(3)

    copies.sent(seven, s_dir)
    copies.sent(pcs, s_pc)
    copies.sent(pys, s_py)
    for each in (gv, gk, sk, sv):
        each.sends()
    copies.sent(kga.at[:, 0:3], s_ky)
    copies.sent(kga.at[:, 0:4], s_kp)

    @pl.when(forward)
    def _():
        for n in range(NQ):
            @pl.when(jnp.logical_not(root) | (n >= NQ - 2))
            def _():
                copies.sent(wpart(n), s_wz + n)

    @pl.when(part)
    def _():
        copies.sent(wzr, s_wx)
        copies.sent(wsum, s_x)
        copies.sent(wfin, s_c)

        @pl.when(root)
        def _():
            copies.sent(wlo, s_l)
            copies.sent(wzr, s_y)

        @pl.when(jnp.logical_not(root))
        def _():
            copies.sent(wsum, s_z)

    @pl.when(jnp.logical_not(part))
    def _():
        copies.sent(wg, s_x)

    for g in range(KVH):
        away_copy(0, g).wait()
        away_copy(1, g).wait()


def rotation_table(tokens):
    freqs = ROPE_BASE ** (-np.arange(HD // 2) * 2.0 / HD)
    angles = np.arange(tokens)[:, None] * freqs[None, :]
    return np.concatenate([np.cos(angles), np.sin(angles)], axis=1).astype(np.float32)


def place_kernel(a, b, c, d, ao, bo, co, do, av, bv, cv, dv, came, went):
    names = ((a, av, ao), (b, bv, bo), (c, cv, co), (d, dv, do))
    first = [pltpu.make_async_copy(src, mid, came.at[n]) for n, (src, mid, dst) in enumerate(names)]
    second = [pltpu.make_async_copy(mid, dst, went.at[n]) for n, (src, mid, dst) in enumerate(names)]
    for cp in first:
        cp.start()
    for one, two in zip(first, second):
        one.wait()
        two.start()
    for cp in second:
        cp.wait()


def local(inputs, queries, values, key_weight, doc_ids, grad_out):
    rows = HD
    width = KVH * HD
    keys = 9 * rows
    table = jnp.asarray(rotation_table(doc_ids.shape[1]))
    vmem = pl.BlockSpec(memory_space=pltpu.VMEM)
    anywhere = pl.BlockSpec(memory_space=pl.ANY)
    dma = pltpu.SemaphoreType.DMA
    V = pltpu.VMEM
    tile = (rows, HD)
    attn, dq, grad_values, weight_grad = pl.pallas_call(
        whole_kernel,
        out_shape=(
            jax.ShapeDtypeStruct((rows, QH * HD), BF),
            jax.ShapeDtypeStruct((rows, QH * HD), BF),
            jax.ShapeDtypeStruct((rows, width), BF),
            jax.ShapeDtypeStruct((384, width), F32),
        ),
        in_specs=[anywhere, anywhere, anywhere, anywhere, anywhere, vmem, anywhere],
        out_specs=(anywhere, anywhere, vmem, vmem),
        scratch_shapes=[
            V((rows, QH * HD), BF),
            V((rows, QH * HD), BF),
            V((rows, QH * HD), BF),
            V((rows, QH * HD), BF),
            V((4, 2, rows, 768), BF),
            V((768, 1024), BF),
            V((2, 384, width), BF),
            V((KVH, 4, 3) + tile, BF),
            V((KVH, 4, 3) + tile, BF),
            V((2, 4, rows, 256), F32),
            V((2, 4, rows, 256), BF),
            V((2, 4, rows, 256), BF),
            V((2, 3, rows, 256), BF),
            V((2, 3, rows, 256), BF),
            V(tile, F32),
            V((GROUP * rows, keys), BF),
            V((GROUP * rows, keys), BF),
            V((2 * rows, keys), F32),
            V((keys, HD), BF),
            V((keys, HD), BF),
            V((GROUP * rows, HD), BF),
            V((GROUP * rows, HD), BF),
            V((KVH, 4, 3) + tile, BF),
            V((KVH, 4, 3) + tile, BF),
            V((KVH, 6) + tile, BF),
            V((KVH, 6) + tile, BF),
            V((KVH, 2) + tile, BF),
            V((KVH, 2) + tile, BF),
            V((KVH, 2) + tile, BF),
            V((KVH, 2) + tile, BF),
            V((KVH, 3) + tile, F32),
            V((KVH, 3) + tile, F32),
            V((KVH, 8) + tile, BF),
            V((KVH, 2, 384, HD), BF),
            V((KVH, 3, 384, HD), BF),
            V((KVH, 384, HD), BF),
            V((KVH, 3, 384, HD), BF),
            V((KVH, 384, HD), BF),
            V((KVH, 384, HD), BF),
            V((KVH, 384, HD), BF),
            dma((SENDS,)),
            dma((RECVS,)),
            dma((17,)),
        ],
        compiler_params=pltpu.CompilerParams(
            collective_id=0, has_side_effects=True, vmem_limit_bytes=VMEM_LIMIT
        ),
        name="whole",
    )(inputs[0], key_weight, values[0], queries[0], grad_out[0], doc_ids, table)
    attn, dq, grad_values, weight_grad = pl.pallas_call(
        place_kernel,
        out_shape=(
            jax.ShapeDtypeStruct((rows, QH * HD), BF),
            jax.ShapeDtypeStruct((rows, QH * HD), BF),
            jax.ShapeDtypeStruct((rows, width), BF),
            jax.ShapeDtypeStruct((384, width), F32),
        ),
        in_specs=[anywhere] * 4,
        out_specs=(anywhere,) * 4,
        scratch_shapes=[
            V((rows, QH * HD), BF),
            V((rows, QH * HD), BF),
            V((rows, width), BF),
            V((384, width), F32),
            dma((4,)),
            dma((4,)),
        ],
        name="place_results",
    )(attn, dq, grad_values, weight_grad)
    return attn[None], dq[None], grad_values[None], weight_grad


def solution(mesh):
    in_specs = (
        P("dp", "seq", None),
        P("dp", "seq", None),
        P("dp", "seq", None),
        P("seq", None),
        P("dp", None),
        P("dp", "seq", None),
    )
    out_specs = (P("dp", "seq", None), P("dp", "seq", None), P("dp", "seq", None), P("seq", None))
    return jax.shard_map(local, mesh=mesh, in_specs=in_specs, out_specs=out_specs, check_vma=False)
```

```python
import math

import jax
import jax.numpy as jnp
import numpy as np
from jax import lax
from jax.experimental import pallas as pl
from jax.experimental.pallas import tpu as pltpu
from jax.sharding import PartitionSpec as P

QH = 24
KVH = 4
HD = 128
GROUP = QH // KVH
ROPE_BASE = 1000000.0
MESH = pl.DeviceIdType.MESH
BF = jnp.bfloat16
F32 = jnp.float32
NQ = 4
SENDS = 20
RECVS = 70
VMEM_LIMIT = 56 * 1024 * 1024


class Place:
    def __init__(self):
        dp = lax.axis_index("dp")
        sq = lax.axis_index("seq")
        self.lo = dp // 8
        self.y = (dp // 2) % 4
        self.c = dp % 2
        self.zh = sq // 4
        self.x = sq % 4
        self.j = dp % 8

    def at(self, lo=None, y=None, c=None, zh=None, x=None):
        lo = self.lo if lo is None else lo
        y = self.y if y is None else y
        c = self.c if c is None else c
        zh = self.zh if zh is None else zh
        x = self.x if x is None else x
        return (lo * 8 + y * 2 + c, zh * 4 + x)

    def z_next(self):
        return self.at(lo=1 - self.lo, zh=(self.zh + self.lo) % 4)

    def z_prev(self):
        return self.at(lo=1 - self.lo, zh=(self.zh + 3 + self.lo) % 4)


class Copies:
    def __init__(self, send, recv, other):
        self.send, self.recv, self.other = send, recv, other
        self.sends = self.recvs = 0

    def new_send(self, number=1):
        self.sends += number
        return self.sends - number

    def new_recv(self, number=1):
        self.recvs += number
        return self.recvs - number

    def make(self, src, dst, send, recv, device):
        return pltpu.make_async_remote_copy(
            src_ref=src,
            dst_ref=dst,
            send_sem=self.send.at[send],
            recv_sem=self.recv.at[recv],
            device_id=device,
            device_id_type=MESH,
        )

    def sent(self, ref, send):
        self.make(ref, ref, send, 0, self.other).wait_send()

    def got(self, ref, recv):
        self.make(ref, ref, 0, recv, self.other).wait_recv()


def greet(devices):
    barrier = pltpu.get_barrier_semaphore()
    for device in devices:
        pl.semaphore_signal(barrier, inc=1, device_id=device, device_id_type=MESH)
    pl.semaphore_wait(barrier, len(devices))


def kind(source, reader):
    return jnp.where(reader > source, 0, 2)


class Gather:
    def __init__(self, place, copies, buf):
        self.p, self.copies, self.buf = place, copies, buf
        self.out = copies.new_send()
        self.base = copies.new_recv(3 * KVH)

    def cp(self, what, g, k, to, device):
        x = self.p.x
        index = self.base + KVH * what + g
        self.copies.make(self.buf.at[g, x, k], self.buf.at[g, x, to], self.out, index, device).start()

    def across(self, g, k):
        p = self.p
        for d in (2, 1, 3):
            to = (p.x + d) % 4
            if k == 1:
                self.cp(2, g, 1, 1, p.at(x=to))
            else:
                @pl.when(kind(p.x, to) == k)
                def _():
                    self.cp(2, g, k, k, p.at(x=to))

    def start(self, g):
        p = self.p
        self.cp(0, g, 0, 1, p.at(zh=(p.zh + 1) % 4))
        self.cp(1, g, 0, 2, p.at(zh=(p.zh + 2) % 4))
        self.across(g, 0)

    def pass_on(self, g):
        for what in (0, 1):
            self.copies.got(self.buf.at[g, self.p.x, what + 1], self.base + KVH * what + g)
            self.across(g, what + 1)

    def end(self, g):
        self.copies.got(self.buf.at[g, 0:2], self.base + 2 * KVH + g)

    def sends(self):
        self.copies.sent(self.buf.at[:, :, 0:2], self.out)


class Scatter:
    def __init__(self, place, copies, buf, rn, rz, zs, acc):
        self.p, self.copies, self.buf = place, copies, buf
        self.rn, self.rz, self.zs, self.acc = rn, rz, zs, acc
        self.out = copies.new_send(2)
        self.base = copies.new_recv(2 * KVH)

    def start(self, g):
        p = self.p
        for d in (2, 1, 3):
            to = (p.x + d) % 4
            for slot, k in ((d - 1, kind(to, p.x)), (2 + d, 1)):
                self.copies.make(
                    self.buf.at[g, to, k], self.rn.at[g, slot], self.out, self.base + g, p.at(x=to)
                ).start()

    def across(self, g):
        p = self.p
        acc = self.acc
        self.copies.got(self.rn.at[g], self.base + g)
        for k in range(3):
            acc[g, k] = self.buf[g, p.x, k].astype(F32)
        for d in (1, 3, 2):
            k = kind(p.x, (p.x + 4 - d) % 4)
            acc[g, k] += self.rn[g, d - 1].astype(F32)
            acc[g, 1] += self.rn[g, 2 + d].astype(F32)
        for n, back in ((1, 2), (0, 3)):
            self.zs[g, n] = acc[g, n + 1].astype(BF)
            self.copies.make(
                self.zs.at[g, n], self.rz.at[g, n], self.out + 1, self.base + KVH + g, p.at(zh=(p.zh + back) % 4)
            ).start()

    def end(self, g):
        self.copies.got(self.rz.at[g], self.base + KVH + g)
        return self.acc[g, 0] + self.rz[g, 0].astype(F32) + self.rz[g, 1].astype(F32)

    def sends(self):
        self.copies.sent(self.rn, self.out)
        self.copies.sent(self.rz, self.out + 1)


def spread(table):
    lane = lax.broadcasted_iota(jnp.int32, table.shape, 1)
    turned = pltpu.roll(table, HD // 2, 1)
    return jnp.where(lane < HD // 2, table, turned), jnp.where(lane < HD // 2, -turned, table)


def rope(part, cosine, sine, sign):
    return part * cosine + sign * (pltpu.roll(part, HD // 2, 1) * sine)


def whole_kernel(
    hid, w, v, q_in, do_in, docs, table,
    out_o, dq_o, gv_o, gw_o,
    q, do, out, dq,
    ha, hat, wb, kb, vb, po, pcs, pcr, pys, pyr, tab,
    probs, ds_all, bias, kc, vc, qs, dos,
    dkb, dvb, krn, vrn, krz, vrz, kzs, vzs, kacc, vacc,
    kga, wg, wxr, wsum, wzr, wlo, wlr, wfin,
    send, recv, loc,
):
    p = Place()
    lo, y, c, zh, x, j = p.lo, p.y, p.c, p.zh, p.x, p.j
    yr, yl, yf = (y + 1) % 4, (y + 3) % 4, (y + 2) % 4
    mate = p.at(c=1 - c)
    copies = Copies(send, recv, mate)
    up_z, down_z = p.z_next(), p.z_prev()
    xs = [(x + d) % 4 for d in (1, 3, 2)]
    peers = [mate]
    for yy in (yr, yl, yf):
        peers += [p.at(y=yy, c=0), p.at(y=yy, c=1)]
    peers += [p.at(x=xx) for xx in xs]
    for d in (1, 2, 3):
        peers += [p.at(zh=(zh + d) % 4), p.at(zh=(zh + d) % 4, lo=1 - lo)]
    peers.append(p.at(lo=1 - lo))
    rows = HD
    scale = 1.0 / math.sqrt(HD)

    part = x // 2 == c
    b = x % 2
    r = (zh - y + 4) % 4
    root = r == 0
    upward = ((r == 0) & (lo == 1)) | (r == 1) | ((r == 2) & (lo == 0))
    forward = part & (r != 2)
    takes = part & jnp.logical_not(root)

    local_w = pltpu.make_async_copy(w, wb.at[b], loc.at[0])
    local_h = pltpu.make_async_copy(hid.at[:, pl.ds(pl.multiple_of(j * 768, 128), 768)], ha.at[y, c], loc.at[1])
    place = pl.multiple_of((zh * 4 + x) * rows, rows)
    local_t = pltpu.make_async_copy(table.at[pl.ds(place, rows), :], tab, loc.at[2])
    local_q = pltpu.make_async_copy(q_in, q, loc.at[3])
    local_do = pltpu.make_async_copy(do_in, do, loc.at[4])
    local_v = [
        pltpu.make_async_copy(v.at[:, g * HD : (g + 1) * HD], vb.at[g, x, 0], loc.at[5 + g]) for g in range(KVH)
    ]

    @pl.when(part & root)
    def _():
        local_w.start()

    local_h.start()
    for cp in local_v:
        cp.start()
    local_t.start()
    local_q.start()
    local_do.start()
    greet(peers)

    def piece(yy, cc):
        return hid.at[:, pl.ds(pl.multiple_of((2 * yy + cc) * 768, 128), 768)]

    s_wz, r_wz = copies.new_send(NQ), copies.new_recv(NQ)
    s_wx, r_wx = copies.new_send(), copies.new_recv()
    wrows = 384 // NQ

    def wpart(n):
        return wb.at[b, pl.ds(n * wrows, wrows), :]

    def w_start(n):
        ref = wpart(n)

        @pl.when(forward & upward)
        def _():
            copies.make(ref, ref, s_wz + n, r_wz + n, up_z).start()

        @pl.when(forward & jnp.logical_not(upward))
        def _():
            copies.make(ref, ref, s_wz + n, r_wz + n, down_z).start()

        @pl.when(part)
        def _():
            for m in (2, 0, 1):
                copies.make(ref, ref, s_wx, r_wx, p.at(x=xs[m])).start()

    @pl.when(part & root)
    def _():
        local_w.wait()
        w_start(0)
        w_start(1)

    seven = hat.at[0:672]
    s_dir, r_dir = copies.new_send(), copies.new_recv()
    group = ((yf, c), (yf, 1 - c), (yr, c), (yr, 1 - c), (yl, c), (yl, 1 - c), (y, 1 - c))
    for yy, cc in group:
        copies.make(piece(yy, cc), ha.at[y, c], s_dir, r_dir, p.at(y=yy, c=cc)).start()

    gv = Gather(p, copies, vb)
    gk = Gather(p, copies, kb)
    for cp in local_v:
        cp.wait()
    gv.start(0)

    @pl.when(part & root)
    def _():
        for n in range(2, NQ):
            copies.sent(wpart(n - 2), s_wz + n - 2)
            w_start(n)

    @pl.when(takes)
    def _():
        for n in range(NQ):
            copies.got(wpart(n), r_wz + n)
            w_start(n)

    @pl.when(part)
    def _():
        copies.got(wb.at[0], r_wx)

    @pl.when(jnp.logical_not(part))
    def _():
        copies.got(wb, r_wx)

    gv.start(1)
    gv.pass_on(0)
    local_h.wait()
    local_t.wait()
    cosine, sine = spread(tab[...])
    s_pc, r_pc = copies.new_send(), copies.new_recv(2)
    s_py, r_py = copies.new_send(), copies.new_recv(2)
    copies.got(seven, r_dir)
    for half in range(2):
        weights = wb[:, :, half * 256 : (half + 1) * 256].reshape(768, 256)
        theirs = jnp.dot(ha[:, 1 - c].reshape(512, 768), weights, preferred_element_type=F32)
        pcs[half] = theirs.astype(BF).reshape(4, rows, 256)
        copies.make(pcs.at[half], pcr.at[half], s_pc, r_pc + half, mate).start()
        po[half] = jnp.dot(ha[:, c].reshape(512, 768), weights, preferred_element_type=F32).reshape(4, rows, 256)
    for half in range(2):
        copies.got(pcr.at[half], r_pc + half)
        for n, yy in enumerate((yf, yr, yl)):
            pys[half, n] = (po[half, yy] + pcr[half, yy].astype(F32)).astype(BF)
            copies.make(pys.at[half, n], pyr.at[half, n], s_py, r_py + half, p.at(y=yy)).start()

    def keys_of(half):
        total = po[half, y] + pcr[half, y].astype(F32)
        copies.got(pyr.at[half], r_py + half)
        for n in range(3):
            total = total + pyr[half, n].astype(F32)
        for n in range(2):
            kb[2 * half + n, x, 0] = rope(total[:, n * HD : (n + 1) * HD], cosine, sine, 1.0).astype(BF)

    gv.start(2)
    gv.start(3)
    gv.pass_on(1)
    keys_of(0)
    gk.start(0)
    keys_of(1)
    gk.start(1)
    gv.pass_on(2)

    position = zh * 4 + x
    own_docs = jnp.broadcast_to(docs[:, pl.ds(place, rows)], (rows, rows)).T
    row = lax.broadcasted_iota(jnp.int32, (rows, rows), 0)
    col = lax.broadcasted_iota(jnp.int32, (rows, rows), 1)
    for n in range(9):
        block = position - 8 + n
        start = pl.multiple_of(jnp.maximum(block, 0) * rows, rows)
        seen = own_docs == docs[:, pl.ds(start, rows)]
        if n == 8:
            seen = seen & (col <= row)
        column = jnp.where(seen, jnp.where(block >= 0, 0.0, -1e30), -1e30)
        bias[:rows, n * rows : (n + 1) * rows] = column
        bias[rows:, n * rows : (n + 1) * rows] = column
    gk.pass_on(0)
    gk.start(2)
    gk.pass_on(1)
    gk.start(3)
    gv.pass_on(3)
    hat[...] = ha[...].reshape(1024, 768).T
    local_q.wait()
    local_do.wait()

    sk = Scatter(p, copies, dkb, krn, krz, kzs, kacc)
    sv = Scatter(p, copies, dvb, vrn, vrz, vzs, vacc)
    s_ky, r_ky = copies.new_send(), copies.new_recv(KVH)

    def key_grad(g):
        cos1, sin1 = spread(tab[...])
        kga[g, j] = rope(sk.end(g), cos1, sin1, -1.0).astype(BF)
        ref = kga.at[g, j]
        for yy, cc in group:
            copies.make(ref, ref, s_ky, r_ky + g, p.at(y=yy, c=cc)).start()

    nt = (((1,), (1,)), ((), ()))
    tn = (((0,), (0,)), ((), ()))

    u = (x - 2 * c + 4) % 4
    s_x, r_x = copies.new_send(), copies.new_recv(KVH)
    s_z, r_z = copies.new_send(), copies.new_recv(KVH)
    s_l, r_l = copies.new_send(), copies.new_recv(KVH)
    s_c = copies.new_send()
    s_y, r_y = copies.new_send(), copies.new_recv(KVH)
    steps = jnp.where(upward, 2 * r + lo - 1, 2 * (4 - r) - lo)
    top = p.at(lo=jnp.where(upward, 1, 0), zh=y)

    def weight_grad(g):
        copies.got(kga.at[g, 0:7], r_ky + g)
        for t in range(2):
            wg[g, t] = jnp.dot(
                hat[t * 384 : (t + 1) * 384, :], kga[g].reshape(1024, HD), preferred_element_type=F32
            ).astype(BF)

            @pl.when(u != t)
            def _():
                d = (u - t + 3) % 4
                copies.make(wg.at[g, t], wxr.at[g, d], s_x, r_x + g, p.at(x=2 * c + t)).start()

    def x_sum(g):
        @pl.when(part)
        def _():
            total = wg[g, b].astype(F32)
            copies.got(wxr.at[g], r_x + g)
            for d in range(3):
                total = total + wxr[g, d].astype(F32)
            wsum[g] = total.astype(BF)

            @pl.when(jnp.logical_not(root))
            def _():
                copies.make(wsum.at[g], wzr.at[g, steps - 1], s_z, r_z + g, top).start()

    def z_sum(g):
        @pl.when(part & root)
        def _():
            total = wsum[g].astype(F32)
            copies.got(wzr.at[g], r_z + g)
            for d in range(3):
                total = total + wzr[g, d].astype(F32)
            wlo[g] = total.astype(BF)
            copies.make(wlo.at[g], wlr.at[g], s_l, r_l + g, p.at(lo=1 - lo)).start()

    def finish(g):
        @pl.when(part & root)
        def _():
            copies.got(wlr.at[g], r_l + g)
            total = wlo[g].astype(F32) + wlr[g].astype(F32)
            wfin[g] = (total * (1.0 / 16.0)).astype(BF)
            for yy in (yf, yr, yl):
                copies.make(wfin.at[g], wfin.at[g], s_y, r_y + g, p.at(y=yy)).start()
            copies.make(wfin.at[g], wfin.at[g], s_c, r_y + g, mate).start()

    def take(g):
        @pl.when(part & jnp.logical_not(root))
        def _():
            copies.got(wfin.at[g], r_y + g)
            copies.make(wfin.at[g], wfin.at[g], s_c, r_y + g, mate).start()

    def keep(g):
        @pl.when(jnp.logical_not(part))
        def _():
            copies.got(wfin.at[g], r_y + g)

        gw_o[:, g * HD : (g + 1) * HD] = wfin[g].astype(F32)

    def value_out(g):
        gv_o[:, g * HD : (g + 1) * HD] = sv.end(g).astype(BF)

    def ready(g):
        gk.end(g)
        gv.end(g)

    def away_copy(n, g):
        at = pl.ds(pl.multiple_of(g * (GROUP * HD), HD), GROUP * HD)
        src, dst = ((out, out_o), (dq, dq_o))[n]
        return pltpu.make_async_copy(src.at[:, at], dst.at[:, at], loc.at[9 + KVH * n + g])

    def head(g, carry):
        ready(g)
        for n in range(9):
            xx, kk = (x + n) % 4, 2 - (x + n) // 4
            kc[n * rows : (n + 1) * rows] = kb[g, xx, kk]
            vc[n * rows : (n + 1) * rows] = vb[g, xx, kk]

        def lanes(h):
            return pl.ds(pl.multiple_of(g * (GROUP * HD) + h * HD, HD), HD)

        for h in range(GROUP):
            qs[h * rows : (h + 1) * rows] = q[:, lanes(h)]
            dos[h * rows : (h + 1) * rows] = do[:, lanes(h)]
        for pair in range(GROUP // 2):
            to = slice(pair * 2 * rows, (pair + 1) * 2 * rows)
            s = lax.dot_general(qs[to], kc[...], nt, preferred_element_type=F32)
            wt = jnp.exp2(s * (scale * math.log2(math.e)) + bias[...])
            inverse = 1.0 / jnp.sum(wt, axis=1, keepdims=True)
            mixed = jnp.dot(wt.astype(BF), vc[...], preferred_element_type=F32)
            attended = (mixed * inverse).astype(BF)
            delta = jnp.sum(dos[to].astype(F32) * attended.astype(F32), axis=1, keepdims=True)
            prob = wt * inverse
            probs[to] = prob.astype(BF)
            dprob = lax.dot_general(dos[to], vc[...], nt, preferred_element_type=F32)
            ds = (prob * (dprob - delta)).astype(BF)
            ds_all[to] = ds
            dquery = (jnp.dot(ds, kc[...], preferred_element_type=F32) * scale).astype(BF)
            for n in range(2):
                out[:, lanes(2 * pair + n)] = attended[n * rows : (n + 1) * rows]
                dq[:, lanes(2 * pair + n)] = dquery[n * rows : (n + 1) * rows]
            if pair == 0:
                @pl.when(g == 0)
                def _():
                    gk.pass_on(2)

                @pl.when(g == 2)
                def _():
                    sk.across(0)

                @pl.when(g >= 2)
                def _():
                    sv.across(g - 2)
            if pair == 1:
                @pl.when(g == 0)
                def _():
                    gk.pass_on(3)

        dkc = (lax.dot_general(qs[...], ds_all[...], tn, preferred_element_type=F32) * scale).astype(BF)
        @pl.when(g >= 2)
        def _():
            sk.across(g - 1)

        for n in range(9):
            dkb[g, (x + n) % 4, 2 - (x + n) // 4] = dkc[:, n * rows : (n + 1) * rows].T
        sk.start(g)

        @pl.when(g >= 2)
        def _():
            key_grad(g - 2)

        dvc = lax.dot_general(dos[...], probs[...], tn, preferred_element_type=F32).astype(BF)
        for n in range(9):
            dvb[g, (x + n) % 4, 2 - (x + n) // 4] = dvc[:, n * rows : (n + 1) * rows].T
        @pl.when(g < KVH - 1)
        def _():
            sv.start(g)

        away_copy(0, g).start()
        away_copy(1, g).start()
        return carry

    lax.fori_loop(0, KVH, head, 0)

    weight_grad(0)
    sk.across(3)
    key_grad(2)
    weight_grad(1)
    x_sum(0)
    sv.across(2)
    key_grad(3)
    x_sum(1)
    weight_grad(2)
    z_sum(0)
    weight_grad(3)
    sv.start(3)
    finish(0)
    x_sum(2)
    z_sum(1)
    x_sum(3)
    finish(1)
    z_sum(2)
    take(0)
    finish(2)
    z_sum(3)
    take(1)
    finish(3)
    take(2)
    sv.across(3)
    keep(0)
    keep(1)
    keep(2)
    take(3)
    for g in range(KVH):
        value_out(g)
    keep(3)

    copies.sent(seven, s_dir)
    copies.sent(pcs, s_pc)
    copies.sent(pys, s_py)
    for each in (gv, gk, sk, sv):
        each.sends()
    copies.sent(kga.at[:, 0:7], s_ky)

    @pl.when(forward)
    def _():
        for n in range(NQ):
            @pl.when(jnp.logical_not(root) | (n >= NQ - 2))
            def _():
                copies.sent(wpart(n), s_wz + n)

    @pl.when(part)
    def _():
        copies.sent(wzr, s_wx)
        copies.sent(wfin, s_x)
        copies.sent(wfin, s_c)

        @pl.when(root)
        def _():
            copies.sent(wlo, s_l)
            copies.sent(wzr, s_y)

        @pl.when(jnp.logical_not(root))
        def _():
            copies.sent(wsum, s_z)

    @pl.when(jnp.logical_not(part))
    def _():
        copies.sent(wg, s_x)

    for g in range(KVH):
        away_copy(0, g).wait()
        away_copy(1, g).wait()


def rotation_table(tokens):
    freqs = ROPE_BASE ** (-np.arange(HD // 2) * 2.0 / HD)
    angles = np.arange(tokens)[:, None] * freqs[None, :]
    return np.concatenate([np.cos(angles), np.sin(angles)], axis=1).astype(np.float32)


def place_kernel(a, b, c, d, ao, bo, co, do, av, bv, cv, dv, came, went):
    names = ((a, av, ao), (b, bv, bo), (c, cv, co), (d, dv, do))
    first = [pltpu.make_async_copy(src, mid, came.at[n]) for n, (src, mid, dst) in enumerate(names)]
    second = [pltpu.make_async_copy(mid, dst, went.at[n]) for n, (src, mid, dst) in enumerate(names)]
    for cp in first:
        cp.start()
    for one, two in zip(first, second):
        one.wait()
        two.start()
    for cp in second:
        cp.wait()


def local(inputs, queries, values, key_weight, doc_ids, grad_out):
    rows = HD
    width = KVH * HD
    keys = 9 * rows
    table = jnp.asarray(rotation_table(doc_ids.shape[1]))
    vmem = pl.BlockSpec(memory_space=pltpu.VMEM)
    anywhere = pl.BlockSpec(memory_space=pl.ANY)
    dma = pltpu.SemaphoreType.DMA
    V = pltpu.VMEM
    tile = (rows, HD)
    attn, dq, grad_values, weight_grad = pl.pallas_call(
        whole_kernel,
        out_shape=(
            jax.ShapeDtypeStruct((rows, QH * HD), BF),
            jax.ShapeDtypeStruct((rows, QH * HD), BF),
            jax.ShapeDtypeStruct((rows, width), BF),
            jax.ShapeDtypeStruct((384, width), F32),
        ),
        in_specs=[anywhere, anywhere, anywhere, anywhere, anywhere, vmem, anywhere],
        out_specs=(anywhere, anywhere, vmem, vmem),
        scratch_shapes=[
            V((rows, QH * HD), BF),
            V((rows, QH * HD), BF),
            V((rows, QH * HD), BF),
            V((rows, QH * HD), BF),
            V((4, 2, rows, 768), BF),
            V((768, 1024), BF),
            V((2, 384, width), BF),
            V((KVH, 4, 3) + tile, BF),
            V((KVH, 4, 3) + tile, BF),
            V((2, 4, rows, 256), F32),
            V((2, 4, rows, 256), BF),
            V((2, 4, rows, 256), BF),
            V((2, 3, rows, 256), BF),
            V((2, 3, rows, 256), BF),
            V(tile, F32),
            V((GROUP * rows, keys), BF),
            V((GROUP * rows, keys), BF),
            V((2 * rows, keys), F32),
            V((keys, HD), BF),
            V((keys, HD), BF),
            V((GROUP * rows, HD), BF),
            V((GROUP * rows, HD), BF),
            V((KVH, 4, 3) + tile, BF),
            V((KVH, 4, 3) + tile, BF),
            V((KVH, 6) + tile, BF),
            V((KVH, 6) + tile, BF),
            V((KVH, 2) + tile, BF),
            V((KVH, 2) + tile, BF),
            V((KVH, 2) + tile, BF),
            V((KVH, 2) + tile, BF),
            V((KVH, 3) + tile, F32),
            V((KVH, 3) + tile, F32),
            V((KVH, 8) + tile, BF),
            V((KVH, 2, 384, HD), BF),
            V((KVH, 3, 384, HD), BF),
            V((KVH, 384, HD), BF),
            V((KVH, 3, 384, HD), BF),
            V((KVH, 384, HD), BF),
            V((KVH, 384, HD), BF),
            V((KVH, 384, HD), BF),
            dma((SENDS,)),
            dma((RECVS,)),
            dma((17,)),
        ],
        compiler_params=pltpu.CompilerParams(
            collective_id=0, has_side_effects=True, vmem_limit_bytes=VMEM_LIMIT
        ),
        name="whole",
    )(inputs[0], key_weight, values[0], queries[0], grad_out[0], doc_ids, table)
    attn, dq, grad_values, weight_grad = pl.pallas_call(
        place_kernel,
        out_shape=(
            jax.ShapeDtypeStruct((rows, QH * HD), BF),
            jax.ShapeDtypeStruct((rows, QH * HD), BF),
            jax.ShapeDtypeStruct((rows, width), BF),
            jax.ShapeDtypeStruct((384, width), F32),
        ),
        in_specs=[anywhere] * 4,
        out_specs=(anywhere,) * 4,
        scratch_shapes=[
            V((rows, QH * HD), BF),
            V((rows, QH * HD), BF),
            V((rows, width), BF),
            V((384, width), F32),
            dma((4,)),
            dma((4,)),
        ],
        name="place_results",
    )(attn, dq, grad_values, weight_grad)
    return attn[None], dq[None], grad_values[None], weight_grad


def solution(mesh):
    in_specs = (
        P("dp", "seq", None),
        P("dp", "seq", None),
        P("dp", "seq", None),
        P("seq", None),
        P("dp", None),
        P("dp", "seq", None),
    )
    out_specs = (P("dp", "seq", None), P("dp", "seq", None), P("dp", "seq", None), P("seq", None))
    return jax.shard_map(local, mesh=mesh, in_specs=in_specs, out_specs=out_specs, check_vma=False)
```

```python
import math

import jax
import jax.numpy as jnp
import numpy as np
from jax import lax
from jax.experimental import pallas as pl
from jax.experimental.pallas import tpu as pltpu
from jax.sharding import PartitionSpec as P

QH = 24
KVH = 4
HD = 128
GROUP = QH // KVH
ROPE_BASE = 1000000.0
MESH = pl.DeviceIdType.MESH
BF = jnp.bfloat16
F32 = jnp.float32
NQ = 8
SENDS = 24
RECVS = 74
VMEM_LIMIT = 56 * 1024 * 1024


class Place:
    def __init__(self):
        dp = lax.axis_index("dp")
        sq = lax.axis_index("seq")
        self.lo = dp // 8
        self.y = (dp // 2) % 4
        self.c = dp % 2
        self.zh = sq // 4
        self.x = sq % 4
        self.j = dp % 8

    def at(self, lo=None, y=None, c=None, zh=None, x=None):
        lo = self.lo if lo is None else lo
        y = self.y if y is None else y
        c = self.c if c is None else c
        zh = self.zh if zh is None else zh
        x = self.x if x is None else x
        return (lo * 8 + y * 2 + c, zh * 4 + x)

    def z_next(self):
        return self.at(lo=1 - self.lo, zh=(self.zh + self.lo) % 4)

    def z_prev(self):
        return self.at(lo=1 - self.lo, zh=(self.zh + 3 + self.lo) % 4)


class Copies:
    def __init__(self, send, recv, other):
        self.send, self.recv, self.other = send, recv, other
        self.sends = self.recvs = 0

    def new_send(self, number=1):
        self.sends += number
        return self.sends - number

    def new_recv(self, number=1):
        self.recvs += number
        return self.recvs - number

    def make(self, src, dst, send, recv, device):
        return pltpu.make_async_remote_copy(
            src_ref=src,
            dst_ref=dst,
            send_sem=self.send.at[send],
            recv_sem=self.recv.at[recv],
            device_id=device,
            device_id_type=MESH,
        )

    def sent(self, ref, send):
        self.make(ref, ref, send, 0, self.other).wait_send()

    def got(self, ref, recv):
        self.make(ref, ref, 0, recv, self.other).wait_recv()


def greet(devices):
    barrier = pltpu.get_barrier_semaphore()
    for device in devices:
        pl.semaphore_signal(barrier, inc=1, device_id=device, device_id_type=MESH)
    pl.semaphore_wait(barrier, len(devices))


def kind(source, reader):
    return jnp.where(reader > source, 0, 2)


class Gather:
    def __init__(self, place, copies, buf):
        self.p, self.copies, self.buf = place, copies, buf
        self.out = copies.new_send()
        self.base = copies.new_recv(3 * KVH)

    def cp(self, what, g, k, to, device):
        x = self.p.x
        index = self.base + KVH * what + g
        self.copies.make(self.buf.at[g, x, k], self.buf.at[g, x, to], self.out, index, device).start()

    def across(self, g, k):
        p = self.p
        for d in (2, 1, 3):
            to = (p.x + d) % 4
            if k == 1:
                self.cp(2, g, 1, 1, p.at(x=to))
            else:
                @pl.when(kind(p.x, to) == k)
                def _():
                    self.cp(2, g, k, k, p.at(x=to))

    def start(self, g):
        p = self.p
        self.cp(0, g, 0, 1, p.at(zh=(p.zh + 1) % 4))
        self.cp(1, g, 0, 2, p.at(zh=(p.zh + 2) % 4))
        self.across(g, 0)

    def pass_on(self, g):
        for what in (0, 1):
            self.copies.got(self.buf.at[g, self.p.x, what + 1], self.base + KVH * what + g)
            self.across(g, what + 1)

    def end(self, g):
        self.copies.got(self.buf.at[g, 0:2], self.base + 2 * KVH + g)

    def sends(self):
        self.copies.sent(self.buf.at[:, :, 0:2], self.out)


class Scatter:
    def __init__(self, place, copies, buf, rn, rz, zs, acc):
        self.p, self.copies, self.buf = place, copies, buf
        self.rn, self.rz, self.zs, self.acc = rn, rz, zs, acc
        self.out = copies.new_send(2)
        self.base = copies.new_recv(2 * KVH)

    def start(self, g):
        p = self.p
        for d in (2, 1, 3):
            to = (p.x + d) % 4
            for slot, k in ((d - 1, kind(to, p.x)), (2 + d, 1)):
                self.copies.make(
                    self.buf.at[g, to, k], self.rn.at[g, slot], self.out, self.base + g, p.at(x=to)
                ).start()

    def across(self, g):
        p = self.p
        acc = self.acc
        self.copies.got(self.rn.at[g], self.base + g)
        for k in range(3):
            acc[g, k] = self.buf[g, p.x, k].astype(F32)
        for d in (1, 3, 2):
            k = kind(p.x, (p.x + 4 - d) % 4)
            acc[g, k] += self.rn[g, d - 1].astype(F32)
            acc[g, 1] += self.rn[g, 2 + d].astype(F32)
        for n, back in ((1, 2), (0, 3)):
            self.zs[g, n] = acc[g, n + 1].astype(BF)
            self.copies.make(
                self.zs.at[g, n], self.rz.at[g, n], self.out + 1, self.base + KVH + g, p.at(zh=(p.zh + back) % 4)
            ).start()

    def end(self, g):
        self.copies.got(self.rz.at[g], self.base + KVH + g)
        return self.acc[g, 0] + self.rz[g, 0].astype(F32) + self.rz[g, 1].astype(F32)

    def sends(self):
        self.copies.sent(self.rn, self.out)
        self.copies.sent(self.rz, self.out + 1)


def spread(table):
    lane = lax.broadcasted_iota(jnp.int32, table.shape, 1)
    turned = pltpu.roll(table, HD // 2, 1)
    return jnp.where(lane < HD // 2, table, turned), jnp.where(lane < HD // 2, -turned, table)


def rope(part, cosine, sine, sign):
    return part * cosine + sign * (pltpu.roll(part, HD // 2, 1) * sine)


def whole_kernel(
    hid, w, v, q_in, do_in, docs, table,
    out_o, dq_o, gv_o, gw_o,
    q, do, out, dq,
    ha, hat, wb, kb, vb, po, pcs, pcr, pys, pyr, tab,
    probs, ds_all, bias, kc, vc, qs, dos,
    dkb, dvb, krn, vrn, krz, vrz, kzs, vzs, kacc, vacc,
    kga, wg, wxr, wsum, wzr, wlo, wlr, wfin,
    send, recv, loc,
):
    p = Place()
    lo, y, c, zh, x, j = p.lo, p.y, p.c, p.zh, p.x, p.j
    yr, yl, yf = (y + 1) % 4, (y + 3) % 4, (y + 2) % 4
    mate = p.at(c=1 - c)
    copies = Copies(send, recv, mate)
    up_z, down_z = p.z_next(), p.z_prev()
    xs = [(x + d) % 4 for d in (1, 3, 2)]
    peers = [mate]
    for yy in (yr, yl, yf):
        peers += [p.at(y=yy, c=0), p.at(y=yy, c=1)]
    peers += [p.at(x=xx) for xx in xs]
    for d in (1, 2, 3):
        peers += [p.at(zh=(zh + d) % 4), p.at(zh=(zh + d) % 4, lo=1 - lo)]
    peers.append(p.at(lo=1 - lo))
    rows = HD
    scale = 1.0 / math.sqrt(HD)

    part = x // 2 == c
    b = x % 2
    r = (zh - y + 4) % 4
    root = r == 0
    upward = ((r == 0) & (lo == 1)) | (r == 1) | ((r == 2) & (lo == 0))
    forward = part & (r != 2)
    takes = part & jnp.logical_not(root)

    local_w = pltpu.make_async_copy(w, wb.at[b], loc.at[0])
    local_h = pltpu.make_async_copy(hid.at[:, pl.ds(pl.multiple_of(j * 768, 128), 768)], ha.at[y, c], loc.at[1])
    place = pl.multiple_of((zh * 4 + x) * rows, rows)
    local_t = pltpu.make_async_copy(table.at[pl.ds(place, rows), :], tab, loc.at[2])
    local_q = pltpu.make_async_copy(q_in, q, loc.at[3])
    local_do = pltpu.make_async_copy(do_in, do, loc.at[4])
    local_v = [
        pltpu.make_async_copy(v.at[:, g * HD : (g + 1) * HD], vb.at[g, x, 0], loc.at[5 + g]) for g in range(KVH)
    ]

    @pl.when(part & root)
    def _():
        local_w.start()

    local_h.start()
    for cp in local_v:
        cp.start()
    local_t.start()
    local_q.start()
    local_do.start()
    greet(peers)

    def piece(yy, cc):
        return hid.at[:, pl.ds(pl.multiple_of((2 * yy + cc) * 768, 128), 768)]

    s_wz, r_wz = copies.new_send(NQ), copies.new_recv(NQ)
    s_wx, r_wx = copies.new_send(), copies.new_recv()
    wrows = 384 // NQ

    def wpart(n):
        return wb.at[b, pl.ds(n * wrows, wrows), :]

    def w_start(n):
        ref = wpart(n)

        @pl.when(forward & upward)
        def _():
            copies.make(ref, ref, s_wz + n, r_wz + n, up_z).start()

        @pl.when(forward & jnp.logical_not(upward))
        def _():
            copies.make(ref, ref, s_wz + n, r_wz + n, down_z).start()

        @pl.when(part)
        def _():
            for m in (2, 0, 1):
                copies.make(ref, ref, s_wx, r_wx, p.at(x=xs[m])).start()

    @pl.when(part & root)
    def _():
        local_w.wait()
        w_start(0)
        w_start(1)

    seven = hat.at[0:672]
    s_dir, r_dir = copies.new_send(), copies.new_recv()
    group = ((yf, c), (yf, 1 - c), (yr, c), (yr, 1 - c), (yl, c), (yl, 1 - c), (y, 1 - c))
    for yy, cc in group:
        copies.make(piece(yy, cc), ha.at[y, c], s_dir, r_dir, p.at(y=yy, c=cc)).start()

    gv = Gather(p, copies, vb)
    gk = Gather(p, copies, kb)
    for cp in local_v:
        cp.wait()
    gv.start(0)

    @pl.when(part & root)
    def _():
        for n in range(2, NQ):
            copies.sent(wpart(n - 2), s_wz + n - 2)
            w_start(n)

    @pl.when(takes)
    def _():
        for n in range(NQ):
            copies.got(wpart(n), r_wz + n)
            w_start(n)

    @pl.when(part)
    def _():
        copies.got(wb.at[0], r_wx)

    @pl.when(jnp.logical_not(part))
    def _():
        copies.got(wb, r_wx)

    gv.start(1)
    gv.pass_on(0)
    local_h.wait()
    local_t.wait()
    cosine, sine = spread(tab[...])
    s_pc, r_pc = copies.new_send(), copies.new_recv(2)
    s_py, r_py = copies.new_send(), copies.new_recv(2)
    copies.got(seven, r_dir)
    for half in range(2):
        weights = wb[:, :, half * 256 : (half + 1) * 256].reshape(768, 256)
        theirs = jnp.dot(ha[:, 1 - c].reshape(512, 768), weights, preferred_element_type=F32)
        pcs[half] = theirs.astype(BF).reshape(4, rows, 256)
        copies.make(pcs.at[half], pcr.at[half], s_pc, r_pc + half, mate).start()
        po[half] = jnp.dot(ha[:, c].reshape(512, 768), weights, preferred_element_type=F32).reshape(4, rows, 256)
    for half in range(2):
        copies.got(pcr.at[half], r_pc + half)
        for n, yy in enumerate((yf, yr, yl)):
            pys[half, n] = (po[half, yy] + pcr[half, yy].astype(F32)).astype(BF)
            copies.make(pys.at[half, n], pyr.at[half, n], s_py, r_py + half, p.at(y=yy)).start()

    def keys_of(half):
        total = po[half, y] + pcr[half, y].astype(F32)
        copies.got(pyr.at[half], r_py + half)
        for n in range(3):
            total = total + pyr[half, n].astype(F32)
        for n in range(2):
            kb[2 * half + n, x, 0] = rope(total[:, n * HD : (n + 1) * HD], cosine, sine, 1.0).astype(BF)

    gv.start(2)
    gv.start(3)
    gv.pass_on(1)
    keys_of(0)
    gk.start(0)
    keys_of(1)
    gk.start(1)
    gv.pass_on(2)

    position = zh * 4 + x
    own_docs = jnp.broadcast_to(docs[:, pl.ds(place, rows)], (rows, rows)).T
    row = lax.broadcasted_iota(jnp.int32, (rows, rows), 0)
    col = lax.broadcasted_iota(jnp.int32, (rows, rows), 1)
    for n in range(9):
        block = position - 8 + n
        start = pl.multiple_of(jnp.maximum(block, 0) * rows, rows)
        seen = own_docs == docs[:, pl.ds(start, rows)]
        if n == 8:
            seen = seen & (col <= row)
        column = jnp.where(seen, jnp.where(block >= 0, 0.0, -1e30), -1e30)
        bias[:rows, n * rows : (n + 1) * rows] = column
        bias[rows:, n * rows : (n + 1) * rows] = column
    gk.pass_on(0)
    gk.start(2)
    gk.pass_on(1)
    gk.start(3)
    gv.pass_on(3)
    hat[...] = ha[...].reshape(1024, 768).T
    local_q.wait()
    local_do.wait()

    sk = Scatter(p, copies, dkb, krn, krz, kzs, kacc)
    sv = Scatter(p, copies, dvb, vrn, vrz, vzs, vacc)
    s_ky, r_ky = copies.new_send(), copies.new_recv(KVH)

    def key_grad(g):
        cos1, sin1 = spread(tab[...])
        kga[g, j] = rope(sk.end(g), cos1, sin1, -1.0).astype(BF)
        ref = kga.at[g, j]
        for yy, cc in group:
            copies.make(ref, ref, s_ky, r_ky + g, p.at(y=yy, c=cc)).start()

    nt = (((1,), (1,)), ((), ()))
    tn = (((0,), (0,)), ((), ()))

    u = (x - 2 * c + 4) % 4
    s_x, r_x = copies.new_send(), copies.new_recv(KVH)
    s_z, r_z = copies.new_send(), copies.new_recv(KVH)
    s_l, r_l = copies.new_send(), copies.new_recv(KVH)
    s_c = copies.new_send()
    s_y, r_y = copies.new_send(), copies.new_recv(KVH)
    steps = jnp.where(upward, 2 * r + lo - 1, 2 * (4 - r) - lo)
    top = p.at(lo=jnp.where(upward, 1, 0), zh=y)

    def weight_grad(g):
        copies.got(kga.at[g, 0:7], r_ky + g)
        for t in range(2):
            wg[g, t] = jnp.dot(
                hat[t * 384 : (t + 1) * 384, :], kga[g].reshape(1024, HD), preferred_element_type=F32
            ).astype(BF)

            @pl.when(u != t)
            def _():
                d = (u - t + 3) % 4
                copies.make(wg.at[g, t], wxr.at[g, d], s_x, r_x + g, p.at(x=2 * c + t)).start()

    def x_sum(g):
        @pl.when(part)
        def _():
            total = wg[g, b].astype(F32)
            copies.got(wxr.at[g], r_x + g)
            for d in range(3):
                total = total + wxr[g, d].astype(F32)
            wsum[g] = total.astype(BF)

            @pl.when(jnp.logical_not(root))
            def _():
                copies.make(wsum.at[g], wzr.at[g, steps - 1], s_z, r_z + g, top).start()

    def z_sum(g):
        @pl.when(part & root)
        def _():
            total = wsum[g].astype(F32)
            copies.got(wzr.at[g], r_z + g)
            for d in range(3):
                total = total + wzr[g, d].astype(F32)
            wlo[g] = total.astype(BF)
            copies.make(wlo.at[g], wlr.at[g], s_l, r_l + g, p.at(lo=1 - lo)).start()

    def finish(g):
        @pl.when(part & root)
        def _():
            copies.got(wlr.at[g], r_l + g)
            total = wlo[g].astype(F32) + wlr[g].astype(F32)
            wfin[g] = (total * (1.0 / 16.0)).astype(BF)
            for yy in (yf, yr, yl):
                copies.make(wfin.at[g], wfin.at[g], s_y, r_y + g, p.at(y=yy)).start()
            copies.make(wfin.at[g], wfin.at[g], s_c, r_y + g, mate).start()

    def take(g):
        @pl.when(part & jnp.logical_not(root))
        def _():
            copies.got(wfin.at[g], r_y + g)
            copies.make(wfin.at[g], wfin.at[g], s_c, r_y + g, mate).start()

    def keep(g):
        @pl.when(jnp.logical_not(part))
        def _():
            copies.got(wfin.at[g], r_y + g)

        gw_o[:, g * HD : (g + 1) * HD] = wfin[g].astype(F32)

    def value_out(g):
        gv_o[:, g * HD : (g + 1) * HD] = sv.end(g).astype(BF)

    def ready(g):
        gk.end(g)
        gv.end(g)

    def away_copy(n, g):
        at = pl.ds(pl.multiple_of(g * (GROUP * HD), HD), GROUP * HD)
        src, dst = ((out, out_o), (dq, dq_o))[n]
        return pltpu.make_async_copy(src.at[:, at], dst.at[:, at], loc.at[9 + KVH * n + g])

    def head(g, carry):
        ready(g)
        for n in range(9):
            xx, kk = (x + n) % 4, 2 - (x + n) // 4
            kc[n * rows : (n + 1) * rows] = kb[g, xx, kk]
            vc[n * rows : (n + 1) * rows] = vb[g, xx, kk]

        def lanes(h):
            return pl.ds(pl.multiple_of(g * (GROUP * HD) + h * HD, HD), HD)

        for h in range(GROUP):
            qs[h * rows : (h + 1) * rows] = q[:, lanes(h)]
            dos[h * rows : (h + 1) * rows] = do[:, lanes(h)]
        for pair in range(GROUP // 2):
            to = slice(pair * 2 * rows, (pair + 1) * 2 * rows)
            s = lax.dot_general(qs[to], kc[...], nt, preferred_element_type=F32)
            wt = jnp.exp2(s * (scale * math.log2(math.e)) + bias[...])
            inverse = 1.0 / jnp.sum(wt, axis=1, keepdims=True)
            mixed = jnp.dot(wt.astype(BF), vc[...], preferred_element_type=F32)
            attended = (mixed * inverse).astype(BF)
            delta = jnp.sum(dos[to].astype(F32) * attended.astype(F32), axis=1, keepdims=True)
            prob = wt * inverse
            probs[to] = prob.astype(BF)
            dprob = lax.dot_general(dos[to], vc[...], nt, preferred_element_type=F32)
            ds = (prob * (dprob - delta)).astype(BF)
            ds_all[to] = ds
            dquery = (jnp.dot(ds, kc[...], preferred_element_type=F32) * scale).astype(BF)
            for n in range(2):
                out[:, lanes(2 * pair + n)] = attended[n * rows : (n + 1) * rows]
                dq[:, lanes(2 * pair + n)] = dquery[n * rows : (n + 1) * rows]
            if pair == 0:
                @pl.when(g == 0)
                def _():
                    gk.pass_on(2)

                @pl.when(g == 2)
                def _():
                    sk.across(0)

                @pl.when(g >= 2)
                def _():
                    sv.across(g - 2)
            if pair == 1:
                @pl.when(g == 0)
                def _():
                    gk.pass_on(3)

        dkc = (lax.dot_general(qs[...], ds_all[...], tn, preferred_element_type=F32) * scale).astype(BF)
        @pl.when(g >= 2)
        def _():
            sk.across(g - 1)

        for n in range(9):
            dkb[g, (x + n) % 4, 2 - (x + n) // 4] = dkc[:, n * rows : (n + 1) * rows].T
        sk.start(g)

        @pl.when(g >= 2)
        def _():
            key_grad(g - 2)

        dvc = lax.dot_general(dos[...], probs[...], tn, preferred_element_type=F32).astype(BF)
        for n in range(9):
            dvb[g, (x + n) % 4, 2 - (x + n) // 4] = dvc[:, n * rows : (n + 1) * rows].T
        @pl.when(g < KVH - 1)
        def _():
            sv.start(g)

        away_copy(0, g).start()
        away_copy(1, g).start()
        return carry

    lax.fori_loop(0, KVH, head, 0)

    weight_grad(0)
    sk.across(3)
    key_grad(2)
    weight_grad(1)
    x_sum(0)
    sv.across(2)
    key_grad(3)
    x_sum(1)
    weight_grad(2)
    z_sum(0)
    weight_grad(3)
    sv.start(3)
    finish(0)
    x_sum(2)
    z_sum(1)
    x_sum(3)
    finish(1)
    z_sum(2)
    take(0)
    finish(2)
    z_sum(3)
    take(1)
    finish(3)
    take(2)
    sv.across(3)
    keep(0)
    keep(1)
    keep(2)
    take(3)
    for g in range(KVH):
        value_out(g)
    keep(3)

    copies.sent(seven, s_dir)
    copies.sent(pcs, s_pc)
    copies.sent(pys, s_py)
    for each in (gv, gk, sk, sv):
        each.sends()
    copies.sent(kga.at[:, 0:7], s_ky)

    @pl.when(forward)
    def _():
        for n in range(NQ):
            @pl.when(jnp.logical_not(root) | (n >= NQ - 2))
            def _():
                copies.sent(wpart(n), s_wz + n)

    @pl.when(part)
    def _():
        copies.sent(wzr, s_wx)
        copies.sent(wfin, s_x)
        copies.sent(wfin, s_c)

        @pl.when(root)
        def _():
            copies.sent(wlo, s_l)
            copies.sent(wzr, s_y)

        @pl.when(jnp.logical_not(root))
        def _():
            copies.sent(wsum, s_z)

    @pl.when(jnp.logical_not(part))
    def _():
        copies.sent(wg, s_x)

    for g in range(KVH):
        away_copy(0, g).wait()
        away_copy(1, g).wait()


def rotation_table(tokens):
    freqs = ROPE_BASE ** (-np.arange(HD // 2) * 2.0 / HD)
    angles = np.arange(tokens)[:, None] * freqs[None, :]
    return np.concatenate([np.cos(angles), np.sin(angles)], axis=1).astype(np.float32)


def place_kernel(a, b, c, d, ao, bo, co, do, av, bv, cv, dv, came, went):
    names = ((a, av, ao), (b, bv, bo), (c, cv, co), (d, dv, do))
    first = [pltpu.make_async_copy(src, mid, came.at[n]) for n, (src, mid, dst) in enumerate(names)]
    second = [pltpu.make_async_copy(mid, dst, went.at[n]) for n, (src, mid, dst) in enumerate(names)]
    for cp in first:
        cp.start()
    for one, two in zip(first, second):
        one.wait()
        two.start()
    for cp in second:
        cp.wait()


def local(inputs, queries, values, key_weight, doc_ids, grad_out):
    rows = HD
    width = KVH * HD
    keys = 9 * rows
    table = jnp.asarray(rotation_table(doc_ids.shape[1]))
    vmem = pl.BlockSpec(memory_space=pltpu.VMEM)
    anywhere = pl.BlockSpec(memory_space=pl.ANY)
    dma = pltpu.SemaphoreType.DMA
    V = pltpu.VMEM
    tile = (rows, HD)
    attn, dq, grad_values, weight_grad = pl.pallas_call(
        whole_kernel,
        out_shape=(
            jax.ShapeDtypeStruct((rows, QH * HD), BF),
            jax.ShapeDtypeStruct((rows, QH * HD), BF),
            jax.ShapeDtypeStruct((rows, width), BF),
            jax.ShapeDtypeStruct((384, width), F32),
        ),
        in_specs=[anywhere, anywhere, anywhere, anywhere, anywhere, vmem, anywhere],
        out_specs=(anywhere, anywhere, vmem, vmem),
        scratch_shapes=[
            V((rows, QH * HD), BF),
            V((rows, QH * HD), BF),
            V((rows, QH * HD), BF),
            V((rows, QH * HD), BF),
            V((4, 2, rows, 768), BF),
            V((768, 1024), BF),
            V((2, 384, width), BF),
            V((KVH, 4, 3) + tile, BF),
            V((KVH, 4, 3) + tile, BF),
            V((2, 4, rows, 256), F32),
            V((2, 4, rows, 256), BF),
            V((2, 4, rows, 256), BF),
            V((2, 3, rows, 256), BF),
            V((2, 3, rows, 256), BF),
            V(tile, F32),
            V((GROUP * rows, keys), BF),
            V((GROUP * rows, keys), BF),
            V((2 * rows, keys), F32),
            V((keys, HD), BF),
            V((keys, HD), BF),
            V((GROUP * rows, HD), BF),
            V((GROUP * rows, HD), BF),
            V((KVH, 4, 3) + tile, BF),
            V((KVH, 4, 3) + tile, BF),
            V((KVH, 6) + tile, BF),
            V((KVH, 6) + tile, BF),
            V((KVH, 2) + tile, BF),
            V((KVH, 2) + tile, BF),
            V((KVH, 2) + tile, BF),
            V((KVH, 2) + tile, BF),
            V((KVH, 3) + tile, F32),
            V((KVH, 3) + tile, F32),
            V((KVH, 8) + tile, BF),
            V((KVH, 2, 384, HD), BF),
            V((KVH, 3, 384, HD), BF),
            V((KVH, 384, HD), BF),
            V((KVH, 3, 384, HD), BF),
            V((KVH, 384, HD), BF),
            V((KVH, 384, HD), BF),
            V((KVH, 384, HD), BF),
            dma((SENDS,)),
            dma((RECVS,)),
            dma((17,)),
        ],
        compiler_params=pltpu.CompilerParams(
            collective_id=0, has_side_effects=True, vmem_limit_bytes=VMEM_LIMIT
        ),
        name="whole",
    )(inputs[0], key_weight, values[0], queries[0], grad_out[0], doc_ids, table)
    attn, dq, grad_values, weight_grad = pl.pallas_call(
        place_kernel,
        out_shape=(
            jax.ShapeDtypeStruct((rows, QH * HD), BF),
            jax.ShapeDtypeStruct((rows, QH * HD), BF),
            jax.ShapeDtypeStruct((rows, width), BF),
            jax.ShapeDtypeStruct((384, width), F32),
        ),
        in_specs=[anywhere] * 4,
        out_specs=(anywhere,) * 4,
        scratch_shapes=[
            V((rows, QH * HD), BF),
            V((rows, QH * HD), BF),
            V((rows, width), BF),
            V((384, width), F32),
            dma((4,)),
            dma((4,)),
        ],
        name="place_results",
    )(attn, dq, grad_values, weight_grad)
    return attn[None], dq[None], grad_values[None], weight_grad


def solution(mesh):
    in_specs = (
        P("dp", "seq", None),
        P("dp", "seq", None),
        P("dp", "seq", None),
        P("seq", None),
        P("dp", None),
        P("dp", "seq", None),
    )
    out_specs = (P("dp", "seq", None), P("dp", "seq", None), P("dp", "seq", None), P("seq", None))
    return jax.shard_map(local, mesh=mesh, in_specs=in_specs, out_specs=out_specs, check_vma=False)
```

```python
import math

import jax
import jax.numpy as jnp
import numpy as np
from jax import lax
from jax.experimental import pallas as pl
from jax.experimental.pallas import tpu as pltpu
from jax.sharding import PartitionSpec as P

QH = 24
KVH = 4
HD = 128
GROUP = QH // KVH
ROPE_BASE = 1000000.0
MESH = pl.DeviceIdType.MESH
BF = jnp.bfloat16
F32 = jnp.float32
NQ = 8
SENDS = 24
RECVS = 74
VMEM_LIMIT = 56 * 1024 * 1024


class Place:
    def __init__(self):
        dp = lax.axis_index("dp")
        sq = lax.axis_index("seq")
        self.lo = dp // 8
        self.y = (dp // 2) % 4
        self.c = dp % 2
        self.zh = sq // 4
        self.x = sq % 4
        self.j = dp % 8

    def at(self, lo=None, y=None, c=None, zh=None, x=None):
        lo = self.lo if lo is None else lo
        y = self.y if y is None else y
        c = self.c if c is None else c
        zh = self.zh if zh is None else zh
        x = self.x if x is None else x
        return (lo * 8 + y * 2 + c, zh * 4 + x)

    def z_next(self):
        return self.at(lo=1 - self.lo, zh=(self.zh + self.lo) % 4)

    def z_prev(self):
        return self.at(lo=1 - self.lo, zh=(self.zh + 3 + self.lo) % 4)


class Copies:
    def __init__(self, send, recv, other):
        self.send, self.recv, self.other = send, recv, other
        self.sends = self.recvs = 0

    def new_send(self, number=1):
        self.sends += number
        return self.sends - number

    def new_recv(self, number=1):
        self.recvs += number
        return self.recvs - number

    def make(self, src, dst, send, recv, device):
        return pltpu.make_async_remote_copy(
            src_ref=src,
            dst_ref=dst,
            send_sem=self.send.at[send],
            recv_sem=self.recv.at[recv],
            device_id=device,
            device_id_type=MESH,
        )

    def sent(self, ref, send):
        self.make(ref, ref, send, 0, self.other).wait_send()

    def got(self, ref, recv):
        self.make(ref, ref, 0, recv, self.other).wait_recv()


def greet(devices):
    barrier = pltpu.get_barrier_semaphore()
    for device in devices:
        pl.semaphore_signal(barrier, inc=1, device_id=device, device_id_type=MESH)
    pl.semaphore_wait(barrier, len(devices))


def kind(source, reader):
    return jnp.where(reader > source, 0, 2)


class Gather:
    def __init__(self, place, copies, buf):
        self.p, self.copies, self.buf = place, copies, buf
        self.out = copies.new_send()
        self.base = copies.new_recv(3 * KVH)

    def cp(self, what, g, k, to, device):
        x = self.p.x
        index = self.base + KVH * what + g
        self.copies.make(self.buf.at[g, x, k], self.buf.at[g, x, to], self.out, index, device).start()

    def across(self, g, k):
        p = self.p
        for d in (2, 1, 3):
            to = (p.x + d) % 4
            if k == 1:
                self.cp(2, g, 1, 1, p.at(x=to))
            else:
                @pl.when(kind(p.x, to) == k)
                def _():
                    self.cp(2, g, k, k, p.at(x=to))

    def start(self, g):
        p = self.p
        self.cp(0, g, 0, 1, p.at(zh=(p.zh + 1) % 4))
        self.cp(1, g, 0, 2, p.at(zh=(p.zh + 2) % 4))
        self.across(g, 0)

    def pass_on(self, g):
        for what in (0, 1):
            self.copies.got(self.buf.at[g, self.p.x, what + 1], self.base + KVH * what + g)
            self.across(g, what + 1)

    def end(self, g):
        self.copies.got(self.buf.at[g, 0:2], self.base + 2 * KVH + g)

    def sends(self):
        self.copies.sent(self.buf.at[:, :, 0:2], self.out)


class Scatter:
    def __init__(self, place, copies, buf, rn, rz, zs, acc):
        self.p, self.copies, self.buf = place, copies, buf
        self.rn, self.rz, self.zs, self.acc = rn, rz, zs, acc
        self.out = copies.new_send(2)
        self.base = copies.new_recv(2 * KVH)

    def start(self, g):
        p = self.p
        for d in (2, 1, 3):
            to = (p.x + d) % 4
            for slot, k in ((d - 1, kind(to, p.x)), (2 + d, 1)):
                self.copies.make(
                    self.buf.at[g, to, k], self.rn.at[g, slot], self.out, self.base + g, p.at(x=to)
                ).start()

    def across(self, g):
        p = self.p
        acc = self.acc
        self.copies.got(self.rn.at[g], self.base + g)
        for k in range(3):
            acc[g, k] = self.buf[g, p.x, k].astype(F32)
        for d in (1, 3, 2):
            k = kind(p.x, (p.x + 4 - d) % 4)
            acc[g, k] += self.rn[g, d - 1].astype(F32)
            acc[g, 1] += self.rn[g, 2 + d].astype(F32)
        for n, back in ((1, 2), (0, 3)):
            self.zs[g, n] = acc[g, n + 1].astype(BF)
            self.copies.make(
                self.zs.at[g, n], self.rz.at[g, n], self.out + 1, self.base + KVH + g, p.at(zh=(p.zh + back) % 4)
            ).start()

    def end(self, g):
        self.copies.got(self.rz.at[g], self.base + KVH + g)
        return self.acc[g, 0] + self.rz[g, 0].astype(F32) + self.rz[g, 1].astype(F32)

    def sends(self):
        self.copies.sent(self.rn, self.out)
        self.copies.sent(self.rz, self.out + 1)


def spread(table):
    lane = lax.broadcasted_iota(jnp.int32, table.shape, 1)
    turned = pltpu.roll(table, HD // 2, 1)
    return jnp.where(lane < HD // 2, table, turned), jnp.where(lane < HD // 2, -turned, table)


def rope(part, cosine, sine, sign):
    return part * cosine + sign * (pltpu.roll(part, HD // 2, 1) * sine)


def whole_kernel(
    hid, w, v, q_in, do_in, docs, table,
    out_o, dq_o, gv_o, gw_o,
    q, do, out, dq,
    ha, hat, wb, kb, vb, po, pcs, pcr, pys, pyr, tab,
    probs, ds_all, bias, kc, vc, qs, dos,
    dkb, dvb, krn, vrn, krz, vrz, kzs, vzs, kacc, vacc,
    kga, wg, wxr, wsum, wzr, wlo, wlr, wfin,
    send, recv, loc,
):
    p = Place()
    lo, y, c, zh, x, j = p.lo, p.y, p.c, p.zh, p.x, p.j
    yr, yl, yf = (y + 1) % 4, (y + 3) % 4, (y + 2) % 4
    mate = p.at(c=1 - c)
    copies = Copies(send, recv, mate)
    up_z, down_z = p.z_next(), p.z_prev()
    xs = [(x + d) % 4 for d in (1, 3, 2)]
    peers = [mate]
    for yy in (yr, yl, yf):
        peers += [p.at(y=yy, c=0), p.at(y=yy, c=1)]
    peers += [p.at(x=xx) for xx in xs]
    for d in (1, 2, 3):
        peers += [p.at(zh=(zh + d) % 4), p.at(zh=(zh + d) % 4, lo=1 - lo)]
    peers.append(p.at(lo=1 - lo))
    rows = HD
    scale = 1.0 / math.sqrt(HD)

    part = x // 2 == c
    b = x % 2
    r = (zh - y + 4) % 4
    root = r == 0
    upward = ((r == 0) & (lo == 1)) | (r == 1) | ((r == 2) & (lo == 0))
    forward = part & (r != 2)
    takes = part & jnp.logical_not(root)

    local_w = pltpu.make_async_copy(w, wb.at[b], loc.at[0])
    local_h = pltpu.make_async_copy(hid.at[:, pl.ds(pl.multiple_of(j * 768, 128), 768)], ha.at[y, c], loc.at[1])
    place = pl.multiple_of((zh * 4 + x) * rows, rows)
    local_t = pltpu.make_async_copy(table.at[pl.ds(place, rows), :], tab, loc.at[2])
    local_q = pltpu.make_async_copy(q_in, q, loc.at[3])
    local_do = pltpu.make_async_copy(do_in, do, loc.at[4])
    local_v = [
        pltpu.make_async_copy(v.at[:, g * HD : (g + 1) * HD], vb.at[g, x, 0], loc.at[5 + g]) for g in range(KVH)
    ]

    @pl.when(part & root)
    def _():
        local_w.start()

    local_h.start()
    for cp in local_v:
        cp.start()
    local_t.start()
    local_q.start()
    local_do.start()
    greet(peers)

    def piece(yy, cc):
        return hid.at[:, pl.ds(pl.multiple_of((2 * yy + cc) * 768, 128), 768)]

    s_wz, r_wz = copies.new_send(NQ), copies.new_recv(NQ)
    s_wx, r_wx = copies.new_send(), copies.new_recv()
    wrows = 384 // NQ

    def wpart(n):
        return wb.at[b, pl.ds(n * wrows, wrows), :]

    def w_start(n):
        ref = wpart(n)

        @pl.when(forward & upward)
        def _():
            copies.make(ref, ref, s_wz + n, r_wz + n, up_z).start()

        @pl.when(forward & jnp.logical_not(upward))
        def _():
            copies.make(ref, ref, s_wz + n, r_wz + n, down_z).start()

        @pl.when(part)
        def _():
            for m in (2, 0, 1):
                copies.make(ref, ref, s_wx, r_wx, p.at(x=xs[m])).start()

    @pl.when(part & root)
    def _():
        local_w.wait()
        w_start(0)
        w_start(1)

    seven = hat.at[0:672]
    s_dir, r_dir = copies.new_send(), copies.new_recv()
    group = ((yf, c), (yf, 1 - c), (yr, c), (yr, 1 - c), (yl, c), (yl, 1 - c), (y, 1 - c))
    for yy, cc in group:
        copies.make(piece(yy, cc), ha.at[y, c], s_dir, r_dir, p.at(y=yy, c=cc)).start()

    gv = Gather(p, copies, vb)
    gk = Gather(p, copies, kb)
    for cp in local_v:
        cp.wait()
    gv.start(0)

    @pl.when(part & root)
    def _():
        for n in range(2, NQ):
            copies.sent(wpart(n - 2), s_wz + n - 2)
            w_start(n)

    @pl.when(takes)
    def _():
        for n in range(NQ):
            copies.got(wpart(n), r_wz + n)
            w_start(n)

    @pl.when(part)
    def _():
        copies.got(wb.at[0], r_wx)

    @pl.when(jnp.logical_not(part))
    def _():
        copies.got(wb, r_wx)

    gv.start(1)
    gv.pass_on(0)
    local_h.wait()
    local_t.wait()
    cosine, sine = spread(tab[...])
    s_pc, r_pc = copies.new_send(), copies.new_recv(2)
    s_py, r_py = copies.new_send(), copies.new_recv(2)
    copies.got(seven, r_dir)
    for half in range(2):
        weights = wb[:, :, half * 256 : (half + 1) * 256].reshape(768, 256)
        theirs = jnp.dot(ha[:, 1 - c].reshape(512, 768), weights, preferred_element_type=F32)
        pcs[half] = theirs.astype(BF).reshape(4, rows, 256)
        copies.make(pcs.at[half], pcr.at[half], s_pc, r_pc + half, mate).start()
        po[half] = jnp.dot(ha[:, c].reshape(512, 768), weights, preferred_element_type=F32).reshape(4, rows, 256)
    for half in range(2):
        copies.got(pcr.at[half], r_pc + half)
        for n, yy in enumerate((yf, yr, yl)):
            pys[half, n] = (po[half, yy] + pcr[half, yy].astype(F32)).astype(BF)
            copies.make(pys.at[half, n], pyr.at[half, n], s_py, r_py + half, p.at(y=yy)).start()

    def keys_of(half):
        total = po[half, y] + pcr[half, y].astype(F32)
        copies.got(pyr.at[half], r_py + half)
        for n in range(3):
            total = total + pyr[half, n].astype(F32)
        for n in range(2):
            kb[2 * half + n, x, 0] = rope(total[:, n * HD : (n + 1) * HD], cosine, sine, 1.0).astype(BF)

    gv.start(2)
    gv.start(3)
    gv.pass_on(1)
    keys_of(0)
    gk.start(0)
    keys_of(1)
    gk.start(1)
    gv.pass_on(2)

    position = zh * 4 + x
    own_docs = jnp.broadcast_to(docs[:, pl.ds(place, rows)], (rows, rows)).T
    row = lax.broadcasted_iota(jnp.int32, (rows, rows), 0)
    col = lax.broadcasted_iota(jnp.int32, (rows, rows), 1)
    for n in range(9):
        block = position - 8 + n
        start = pl.multiple_of(jnp.maximum(block, 0) * rows, rows)
        seen = own_docs == docs[:, pl.ds(start, rows)]
        if n == 8:
            seen = seen & (col <= row)
        column = jnp.where(seen, jnp.where(block >= 0, 0.0, -1e30), -1e30)
        bias[:rows, n * rows : (n + 1) * rows] = column
        bias[rows:, n * rows : (n + 1) * rows] = column
    gk.pass_on(0)
    gk.start(2)
    gk.pass_on(1)
    gk.start(3)
    gv.pass_on(3)
    hat[...] = ha[...].reshape(1024, 768).T
    local_q.wait()
    local_do.wait()

    sk = Scatter(p, copies, dkb, krn, krz, kzs, kacc)
    sv = Scatter(p, copies, dvb, vrn, vrz, vzs, vacc)
    s_ky, r_ky = copies.new_send(), copies.new_recv(KVH)

    def key_grad(g):
        cos1, sin1 = spread(tab[...])
        kga[g, j] = rope(sk.end(g), cos1, sin1, -1.0).astype(BF)
        ref = kga.at[g, j]
        for yy, cc in group:
            copies.make(ref, ref, s_ky, r_ky + g, p.at(y=yy, c=cc)).start()

    nt = (((1,), (1,)), ((), ()))
    tn = (((0,), (0,)), ((), ()))

    u = (x - 2 * c + 4) % 4
    s_x, r_x = copies.new_send(), copies.new_recv(KVH)
    s_z, r_z = copies.new_send(), copies.new_recv(KVH)
    s_l, r_l = copies.new_send(), copies.new_recv(KVH)
    s_c = copies.new_send()
    s_y, r_y = copies.new_send(), copies.new_recv(KVH)
    steps = jnp.where(upward, 2 * r + lo - 1, 2 * (4 - r) - lo)
    top = p.at(lo=jnp.where(upward, 1, 0), zh=y)

    def weight_grad(g):
        copies.got(kga.at[g, 0:7], r_ky + g)
        for t in range(2):
            wg[g, t] = jnp.dot(
                hat[t * 384 : (t + 1) * 384, :], kga[g].reshape(1024, HD), preferred_element_type=F32
            ).astype(BF)

            @pl.when(u != t)
            def _():
                d = (u - t + 3) % 4
                copies.make(wg.at[g, t], wxr.at[g, d], s_x, r_x + g, p.at(x=2 * c + t)).start()

    def x_sum(g):
        @pl.when(part)
        def _():
            total = wg[g, b].astype(F32)
            copies.got(wxr.at[g], r_x + g)
            for d in range(3):
                total = total + wxr[g, d].astype(F32)
            wsum[g] = total.astype(BF)

            @pl.when(jnp.logical_not(root))
            def _():
                copies.make(wsum.at[g], wzr.at[g, steps - 1], s_z, r_z + g, top).start()

    def z_sum(g):
        @pl.when(part & root)
        def _():
            total = wsum[g].astype(F32)
            copies.got(wzr.at[g], r_z + g)
            for d in range(3):
                total = total + wzr[g, d].astype(F32)
            wlo[g] = total.astype(BF)
            copies.make(wlo.at[g], wlr.at[g], s_l, r_l + g, p.at(lo=1 - lo)).start()

    def finish(g):
        @pl.when(part & root)
        def _():
            copies.got(wlr.at[g], r_l + g)
            total = wlo[g].astype(F32) + wlr[g].astype(F32)
            wfin[g] = (total * (1.0 / 16.0)).astype(BF)
            for yy in (yf, yr, yl):
                copies.make(wfin.at[g], wfin.at[g], s_y, r_y + g, p.at(y=yy)).start()
            copies.make(wfin.at[g], wfin.at[g], s_c, r_y + g, mate).start()

    def take(g):
        @pl.when(part & jnp.logical_not(root))
        def _():
            copies.got(wfin.at[g], r_y + g)
            copies.make(wfin.at[g], wfin.at[g], s_c, r_y + g, mate).start()

    def keep(g):
        @pl.when(jnp.logical_not(part))
        def _():
            copies.got(wfin.at[g], r_y + g)

        gw_o[:, g * HD : (g + 1) * HD] = wfin[g].astype(F32)

    def value_out(g):
        gv_o[:, g * HD : (g + 1) * HD] = sv.end(g).astype(BF)

    def ready(g):
        gk.end(g)
        gv.end(g)

    def away_copy(n, g):
        at = pl.ds(pl.multiple_of(g * (GROUP * HD), HD), GROUP * HD)
        src, dst = ((out, out_o), (dq, dq_o))[n]
        return pltpu.make_async_copy(src.at[:, at], dst.at[:, at], loc.at[9 + KVH * n + g])

    def head(g, carry):
        ready(g)
        for n in range(9):
            xx, kk = (x + n) % 4, 2 - (x + n) // 4
            kc[n * rows : (n + 1) * rows] = kb[g, xx, kk]
            vc[n * rows : (n + 1) * rows] = vb[g, xx, kk]

        def lanes(h):
            return pl.ds(pl.multiple_of(g * (GROUP * HD) + h * HD, HD), HD)

        for h in range(GROUP):
            qs[h * rows : (h + 1) * rows] = q[:, lanes(h)]
            dos[h * rows : (h + 1) * rows] = do[:, lanes(h)]
        for pair in range(GROUP // 2):
            to = slice(pair * 2 * rows, (pair + 1) * 2 * rows)
            s = lax.dot_general(qs[to], kc[...], nt, preferred_element_type=F32)
            wt = jnp.exp2(s * (scale * math.log2(math.e)) + bias[...])
            inverse = 1.0 / jnp.sum(wt, axis=1, keepdims=True)
            mixed = jnp.dot(wt.astype(BF), vc[...], preferred_element_type=F32)
            attended = (mixed * inverse).astype(BF)
            delta = jnp.sum(dos[to].astype(F32) * attended.astype(F32), axis=1, keepdims=True)
            prob = wt * inverse
            probs[to] = prob.astype(BF)
            dprob = lax.dot_general(dos[to], vc[...], nt, preferred_element_type=F32)
            ds = (prob * (dprob - delta)).astype(BF)
            ds_all[to] = ds
            dquery = (jnp.dot(ds, kc[...], preferred_element_type=F32) * scale).astype(BF)
            for n in range(2):
                out[:, lanes(2 * pair + n)] = attended[n * rows : (n + 1) * rows]
                dq[:, lanes(2 * pair + n)] = dquery[n * rows : (n + 1) * rows]
            if pair == 0:
                @pl.when(g == 0)
                def _():
                    gk.pass_on(2)

                @pl.when(g == 2)
                def _():
                    sk.across(0)

                @pl.when(g >= 2)
                def _():
                    sv.across(g - 2)
            if pair == 1:
                @pl.when(g == 0)
                def _():
                    gk.pass_on(3)

        dkc = (lax.dot_general(qs[...], ds_all[...], tn, preferred_element_type=F32) * scale).astype(BF)
        @pl.when(g >= 2)
        def _():
            sk.across(g - 1)

        for n in range(9):
            dkb[g, (x + n) % 4, 2 - (x + n) // 4] = dkc[:, n * rows : (n + 1) * rows].T
        sk.start(g)

        @pl.when(g >= 2)
        def _():
            key_grad(g - 2)

        dvc = lax.dot_general(dos[...], probs[...], tn, preferred_element_type=F32).astype(BF)
        for n in range(9):
            dvb[g, (x + n) % 4, 2 - (x + n) // 4] = dvc[:, n * rows : (n + 1) * rows].T
        @pl.when(g < KVH - 1)
        def _():
            sv.start(g)

        away_copy(0, g).start()
        away_copy(1, g).start()
        return carry

    lax.fori_loop(0, KVH, head, 0)

    weight_grad(0)
    sk.across(3)
    key_grad(2)
    weight_grad(1)
    x_sum(0)
    sv.across(2)
    key_grad(3)
    x_sum(1)
    weight_grad(2)
    z_sum(0)
    weight_grad(3)
    sv.start(3)
    finish(0)
    x_sum(2)
    z_sum(1)
    x_sum(3)
    finish(1)
    z_sum(2)
    take(0)
    finish(2)
    z_sum(3)
    take(1)
    finish(3)
    take(2)
    sv.across(3)
    keep(0)
    keep(1)
    keep(2)
    take(3)
    for g in range(KVH):
        value_out(g)
    keep(3)

    copies.sent(seven, s_dir)
    copies.sent(pcs, s_pc)
    copies.sent(pys, s_py)
    for each in (gv, gk, sk, sv):
        each.sends()
    copies.sent(kga.at[:, 0:7], s_ky)

    @pl.when(forward)
    def _():
        for n in range(NQ):
            @pl.when(jnp.logical_not(root) | (n >= NQ - 2))
            def _():
                copies.sent(wpart(n), s_wz + n)

    @pl.when(part)
    def _():
        copies.sent(wzr, s_wx)
        copies.sent(wfin, s_x)
        copies.sent(wfin, s_c)

        @pl.when(root)
        def _():
            copies.sent(wlo, s_l)
            copies.sent(wzr, s_y)

        @pl.when(jnp.logical_not(root))
        def _():
            copies.sent(wsum, s_z)

    @pl.when(jnp.logical_not(part))
    def _():
        copies.sent(wg, s_x)

    for g in range(KVH):
        away_copy(0, g).wait()
        away_copy(1, g).wait()


def rotation_table(tokens):
    freqs = ROPE_BASE ** (-np.arange(HD // 2) * 2.0 / HD)
    angles = np.arange(tokens)[:, None] * freqs[None, :]
    return np.concatenate([np.cos(angles), np.sin(angles)], axis=1).astype(np.float32)


def place_kernel(a, b, c, d, ao, bo, co, do, av, bv, cv, dv, came, went):
    names = []
    for n in range(4):
        cols = pl.ds(n * (QH * HD // 4), QH * HD // 4)
        names += [tuple(r.at[:, cols] for r in (a, av, ao)), tuple(r.at[:, cols] for r in (b, bv, bo))]
    for n in range(4):
        names.append(tuple(r.at[pl.ds(n * 96, 96), :] for r in (d, dv, do)))
    names.append((c, cv, co))
    first = [pltpu.make_async_copy(src, mid, came.at[n]) for n, (src, mid, dst) in enumerate(names)]
    second = [pltpu.make_async_copy(mid, dst, went.at[n]) for n, (src, mid, dst) in enumerate(names)]
    for cp in first:
        cp.start()
    for one, two in zip(first, second):
        one.wait()
        two.start()
    for cp in second:
        cp.wait()


def local(inputs, queries, values, key_weight, doc_ids, grad_out):
    rows = HD
    width = KVH * HD
    keys = 9 * rows
    table = jnp.asarray(rotation_table(doc_ids.shape[1]))
    vmem = pl.BlockSpec(memory_space=pltpu.VMEM)
    anywhere = pl.BlockSpec(memory_space=pl.ANY)
    dma = pltpu.SemaphoreType.DMA
    V = pltpu.VMEM
    tile = (rows, HD)
    attn, dq, grad_values, weight_grad = pl.pallas_call(
        whole_kernel,
        out_shape=(
            jax.ShapeDtypeStruct((rows, QH * HD), BF),
            jax.ShapeDtypeStruct((rows, QH * HD), BF),
            jax.ShapeDtypeStruct((rows, width), BF),
            jax.ShapeDtypeStruct((384, width), F32),
        ),
        in_specs=[anywhere, anywhere, anywhere, anywhere, anywhere, vmem, anywhere],
        out_specs=(anywhere, anywhere, vmem, vmem),
        scratch_shapes=[
            V((rows, QH * HD), BF),
            V((rows, QH * HD), BF),
            V((rows, QH * HD), BF),
            V((rows, QH * HD), BF),
            V((4, 2, rows, 768), BF),
            V((768, 1024), BF),
            V((2, 384, width), BF),
            V((KVH, 4, 3) + tile, BF),
            V((KVH, 4, 3) + tile, BF),
            V((2, 4, rows, 256), F32),
            V((2, 4, rows, 256), BF),
            V((2, 4, rows, 256), BF),
            V((2, 3, rows, 256), BF),
            V((2, 3, rows, 256), BF),
            V(tile, F32),
            V((GROUP * rows, keys), BF),
            V((GROUP * rows, keys), BF),
            V((2 * rows, keys), F32),
            V((keys, HD), BF),
            V((keys, HD), BF),
            V((GROUP * rows, HD), BF),
            V((GROUP * rows, HD), BF),
            V((KVH, 4, 3) + tile, BF),
            V((KVH, 4, 3) + tile, BF),
            V((KVH, 6) + tile, BF),
            V((KVH, 6) + tile, BF),
            V((KVH, 2) + tile, BF),
            V((KVH, 2) + tile, BF),
            V((KVH, 2) + tile, BF),
            V((KVH, 2) + tile, BF),
            V((KVH, 3) + tile, F32),
            V((KVH, 3) + tile, F32),
            V((KVH, 8) + tile, BF),
            V((KVH, 2, 384, HD), BF),
            V((KVH, 3, 384, HD), BF),
            V((KVH, 384, HD), BF),
            V((KVH, 3, 384, HD), BF),
            V((KVH, 384, HD), BF),
            V((KVH, 384, HD), BF),
            V((KVH, 384, HD), BF),
            dma((SENDS,)),
            dma((RECVS,)),
            dma((17,)),
        ],
        compiler_params=pltpu.CompilerParams(
            collective_id=0, has_side_effects=True, vmem_limit_bytes=VMEM_LIMIT
        ),
        name="whole",
    )(inputs[0], key_weight, values[0], queries[0], grad_out[0], doc_ids, table)
    attn, dq, grad_values, weight_grad = pl.pallas_call(
        place_kernel,
        out_shape=(
            jax.ShapeDtypeStruct((rows, QH * HD), BF),
            jax.ShapeDtypeStruct((rows, QH * HD), BF),
            jax.ShapeDtypeStruct((rows, width), BF),
            jax.ShapeDtypeStruct((384, width), F32),
        ),
        in_specs=[anywhere] * 4,
        out_specs=(anywhere,) * 4,
        scratch_shapes=[
            V((rows, QH * HD), BF),
            V((rows, QH * HD), BF),
            V((rows, width), BF),
            V((384, width), F32),
            dma((13,)),
            dma((13,)),
        ],
        name="place_results",
    )(attn, dq, grad_values, weight_grad)
    return attn[None], dq[None], grad_values[None], weight_grad


def solution(mesh):
    in_specs = (
        P("dp", "seq", None),
        P("dp", "seq", None),
        P("dp", "seq", None),
        P("seq", None),
        P("dp", None),
        P("dp", "seq", None),
    )
    out_specs = (P("dp", "seq", None), P("dp", "seq", None), P("dp", "seq", None), P("seq", None))
    return jax.shard_map(local, mesh=mesh, in_specs=in_specs, out_specs=out_specs, check_vma=False)
```
